256 devices in a mesh: img: 16 (over z, core), pos: 16 (over x, y).
Axes of the slice: x: 4, y: 4, z: 8, core: 2. Of those that a mesh axis runs over, the one named last changes fastest.
Arguments:
- section_one: bfloat16 [512, 28, 28, 64], P(('img', 'pos')), may hold values from -6 to 6
- section_two: bfloat16 [512, 14, 14, 128], P(('img', 'pos')), may hold values from -6 to 6
- section_three: bfloat16 [512, 7, 7, 256], P(('img', 'pos')), may hold values from -6 to 6
- weight_one: bfloat16 [3, 3, 64, 64], replicated, may hold values from -0.25 to 0.25
- weight_two: bfloat16 [3, 3, 128, 128], replicated, may hold values from -0.1875 to 0.1875
- weight_three: bfloat16 [3, 3, 256, 256], replicated, may hold values from -0.125 to 0.125
- gain_one: float32 [64], replicated, may hold values from 0.25 to 1.75
- gain_two: float32 [128], replicated, may hold values from 0.25 to 1.75
- gain_three: float32 [256], replicated, may hold values from 0.25 to 1.75
- bias_one: float32 [64], replicated, may hold values from -3 to 3
- bias_two: float32 [128], replicated, may hold values from -3 to 3
- bias_three: float32 [256], replicated, may hold values from -3 to 3
- channel_index: int32 [100], replicated, may hold values from 0 to 447, as said below
- valid_count: int32 [16, 16], P('img', 'pos'), may hold values from 1 to 2, as said below
Outputs:
- mean: float32 [100, 784], P(None, 'pos')
- covariance: float32 [784, 10000], P('pos')
The draws below stay inside these ranges and needn't reach their ends.
Inputs may be any that keep to these rules, and one draw needn't show every extreme that they name: `channel_index`: 100 distinct channel numbers; 0 and 447 are always among them. `valid_count`: A device's valid images are its first slots. Every draw has a device with 2 valid images and one with 1.
All inputs are finite; a program needn't handle non-finite values.
Results may differ from the reference program's by a relative error of at most 0.0022.
Values may be sent and summed in bfloat16 or wider, within the bound.
A program may use at most 128 MiB of HBM per device.

```python
import jax
import jax.numpy as jnp
from jax import lax

C1 = 64
C2 = 128
C3 = 256
CH = 448
K = 100
H1 = 28
H2 = 14
H3 = 7
POSITIONS = 784
IMG_DEV = 2
GROUPS = 16
OWNERS = 16
IMAGES = 512


def draw_channel_index(key, part):
    pick_key, order_key = jax.random.split(key)
    inner = jax.random.permutation(pick_key, CH - 2)[:K - 2] + 1
    chosen = jnp.concatenate([jnp.array([0, CH - 1], jnp.int32), inner.astype(jnp.int32)])
    return chosen[jax.random.permutation(order_key, K)].astype(jnp.int32)


def draw_valid_count(key, part):
    level_key, noise_key, place_key, other_key = jax.random.split(key, 4)
    level = jax.random.randint(level_key, (GROUPS, 1), 1, IMG_DEV + 1)
    noise = jax.random.randint(noise_key, (GROUPS, OWNERS), -1, 2)
    counts = jnp.clip(level + noise, 1, IMG_DEV).reshape(-1)
    cells = GROUPS * OWNERS
    full_at = jax.random.randint(place_key, (), 0, cells)
    low_at = (full_at + 1 + jax.random.randint(other_key, (), 0, cells - 1)) % cells
    counts = counts.at[full_at].set(IMG_DEV).at[low_at].set(1)
    return counts.reshape(GROUPS, OWNERS).astype(jnp.int32)


def block_levels(rng, extent, shards, least, top_value):
    def one(dim, parts):
        draws = jax.random.uniform(jax.random.fold_in(jax.random.fold_in(rng, 6), dim), (parts,), jnp.float32, least / len(shards), top_value / len(shards))
        return jnp.repeat(jnp.exp(draws), extent[dim] // parts).reshape((-1,) + (1,) * (len(extent) - dim - 1))

    level = one(*shards[0])
    for cut in shards[1:]:
        level = level * one(*cut)
    return level


def normal_values(stream_key, shape, spread, limit, shards=(), held_as=jnp.bfloat16):
    drawn = jax.random.normal(stream_key, shape, jnp.float32) * spread
    if len(shards) > 0:
        drawn = block_levels(stream_key, shape, shards, -0.22, 0.18) * drawn
    return jnp.clip(drawn, min=-limit, max=limit).astype(held_as)


def setup_inputs(seed: int = 0) -> dict:
    arg_keys = jax.random.split(jax.random.key(seed), 15)
    return {
        "section_one": normal_values(arg_keys[0], (IMAGES, H1, H1, C1), 1.0, 6.0, ((0, 256),)),
        "section_two": normal_values(arg_keys[1], (IMAGES, H2, H2, C2), 1.0, 6.0, ((0, 256),)),
        "section_three": normal_values(arg_keys[2], (IMAGES, H3, H3, C3), 1.0, 6.0, ((0, 256),)),
        "weight_one": normal_values(arg_keys[3], (3, 3, C1, C1), (9 * C1) ** -0.5, 0.25),
        "weight_two": normal_values(arg_keys[4], (3, 3, C2, C2), (9 * C2) ** -0.5, 0.1875),
        "weight_three": normal_values(arg_keys[5], (3, 3, C3, C3), (9 * C3) ** -0.5, 0.125),
        "gain_one": jnp.clip(1.0 + 0.15 * jax.random.normal(arg_keys[6], (C1,), jnp.float32), 0.25, 1.75),
        "gain_two": jnp.clip(1.0 + 0.15 * jax.random.normal(arg_keys[7], (C2,), jnp.float32), 0.25, 1.75),
        "gain_three": jnp.clip(1.0 + 0.15 * jax.random.normal(arg_keys[8], (C3,), jnp.float32), 0.25, 1.75),
        "bias_one": normal_values(arg_keys[9], (C1,), 0.5, 3.0, (), jnp.float32),
        "bias_two": normal_values(arg_keys[10], (C2,), 0.5, 3.0, (), jnp.float32),
        "bias_three": normal_values(arg_keys[11], (C3,), 0.5, 3.0, (), jnp.float32),
        "channel_index": draw_channel_index(jax.random.fold_in(arg_keys[14], 71), 0),
        "valid_count": draw_valid_count(jax.random.fold_in(arg_keys[14], 71), 0),
    }


def section_out(images, weight, gain, bias):
    conv = lax.conv_general_dilated(images.astype(jnp.float32), weight.astype(jnp.float32), (1, 1), "SAME", dimension_numbers=("NHWC", "HWIO", "NHWC"), precision=lax.Precision.HIGHEST)
    return jax.nn.relu(conv * gain + bias).astype(jnp.bfloat16)


def pick_channels(section, offset, width, channel_index):
    table = (channel_index[None, :] - offset == jnp.arange(width, dtype=jnp.int32)[:, None]).astype(jnp.float32)
    return jnp.einsum("ihwc,ck->ikhw", section.astype(jnp.float32), table).astype(jnp.bfloat16)


def widen(picked, factor):
    return jnp.repeat(jnp.repeat(picked, factor, axis=2), factor, axis=3)


def reference(section_one, section_two, section_three, weight_one, weight_two, weight_three, gain_one, gain_two, gain_three, bias_one, bias_two, bias_three, channel_index, valid_count):
    per_block = IMG_DEV * OWNERS
    image_ids = jnp.arange(IMAGES, dtype=jnp.int32)
    flat_counts = valid_count.reshape(-1)
    valid = (image_ids % IMG_DEV < flat_counts[image_ids // IMG_DEV]).astype(jnp.float32)
    total = jnp.sum(valid)

    def accumulate(carry, inputs):
        sums, raw = carry
        first, second, third, valid_rows = inputs
        scale = valid_rows.astype(jnp.bfloat16)[:, None, None, None]
        out_one = section_out(first, weight_one, gain_one, bias_one) * scale
        out_two = section_out(second, weight_two, gain_two, bias_two) * scale
        out_three = section_out(third, weight_three, gain_three, bias_three) * scale
        features = pick_channels(out_one, 0, C1, channel_index)
        features = features + widen(pick_channels(out_two, C1, C2, channel_index), 2)
        features = features + widen(pick_channels(out_three, C1 + C2, C3, channel_index), 4)
        values = features.reshape(per_block, K, POSITIONS).astype(jnp.float32)
        sums = sums + jnp.sum(values, axis=0)
        raw = raw + jnp.einsum("ikp,ilp->pkl", values, values).reshape(POSITIONS, K * K)
        return (sums, raw), None

    inputs = (section_one.reshape(GROUPS, per_block, H1, H1, C1), section_two.reshape(GROUPS, per_block, H2, H2, C2), section_three.reshape(GROUPS, per_block, H3, H3, C3), valid.reshape(GROUPS, per_block))
    start = (jnp.zeros((K, POSITIONS), jnp.float32), jnp.zeros((POSITIONS, K * K), jnp.float32))
    (sums, raw), unused = lax.scan(accumulate, start, inputs)
    mean = sums / total
    turned = mean.T
    moment = raw - total * (turned[:, :, None] * turned[:, None, :]).reshape(POSITIONS, K * K)
    covariance = moment / (total - 1.0) + 0.01 * jnp.eye(K, dtype=jnp.float32).reshape(1, K * K)
    return mean, covariance
```

```python
import functools

import jax
import jax.numpy as jnp
import numpy as np
from jax import lax
from jax.experimental import pallas as pl
from jax.experimental.pallas import tpu as pltpu
from jax.sharding import PartitionSpec as P

MESH = pl.DeviceIdType.MESH
LANES = 128
ONES = 127
SLOTS = 4
UNIT = 8
FLAT = 80
WINDOW = 320


def section_out(images, weight, gain, bias):
    conv = lax.conv_general_dilated(
        images,
        weight,
        (1, 1),
        "SAME",
        dimension_numbers=("NHWC", "HWIO", "NHWC"),
        preferred_element_type=jnp.float32,
    )
    return jax.nn.relu(conv * gain + bias).astype(jnp.bfloat16)


def pick_channels(section, offset, slots):
    width = section.shape[3]
    table = (slots[None, :] - offset == lax.iota(jnp.int32, width)[:, None]).astype(jnp.bfloat16)
    return jnp.einsum(
        "ihwc,ck->ihwk", section, table, preferred_element_type=jnp.float32
    ).astype(jnp.bfloat16)


def gather_table(side, blocks, sharers):
    block = side * side // blocks
    own = block // sharers
    table = np.zeros((blocks, sharers * UNIT, WINDOW), np.float32)
    for j in range(blocks):
        y0 = j * block // side
        for i in range(sharers):
            for q in range(SLOTS):
                position = j * block + (i * own + q if q < own else block - 1)
                y, x = divmod(position, side)
                for g in range(2):
                    row = i * UNIT + q * 2 + g
                    table[j, row, g * 96 + (y - y0) * 32 + x] = 1
                    table[j, row, 192 + g * 32 + (y // 2 - y0 // 2) * 16 + x // 2] = 1
                    table[j, row, 256 + g * 32 + (y // 4 - y0 // 4) * 16 + x // 4] = 1
    return table.astype(jnp.bfloat16)


def iota(shape, dim):
    return lax.broadcasted_iota(jnp.int32, shape, dim)


def flatten_tables(kept):
    f = iota((FLAT, LANES), 0) * LANES
    k = iota((FLAT, LANES), 1)
    picks, masks = [], []
    start = jnp.floor((f.astype(jnp.float32) + 0.5) * (1.0 / kept))
    rest = f - start.astype(jnp.int32) * kept + k
    for t in range(3):
        picks.append(((k - t) * kept <= f) & (f < (k - t + 1) * kept))
        masks.append((rest >= t * kept) & (rest < (t + 1) * kept))
    return jnp.concatenate(picks, 0), masks


def kernel(
    kept,
    f1_ref,
    f2_ref,
    f3_ref,
    table_ref,
    out_ref,
    last_ref,
    s_ref,
    r1_ref,
    r2_ref,
    a_send,
    a_recv,
    b_send,
    b_recv,
    cw_send,
    cw_recv,
    ccw_send,
    ccw_recv,
    pair_send,
    pair_recv,
):
    groups, owners = s_ref.shape[:2]
    chips = groups // 2
    me = lax.axis_index("img")
    my_pos = lax.axis_index("pos")
    z, core = me // 2, me % 2

    barrier = pltpu.get_barrier_semaphore()

    @pl.loop(1, groups)
    def _(d):
        pl.semaphore_signal(
            barrier, inc=1, device_id=(lax.rem(me + d, groups), my_pos), device_id_type=MESH
        )

    @pl.loop(1, owners)
    def _(d):
        pl.semaphore_signal(
            barrier, inc=1, device_id=(me, lax.rem(my_pos + d, owners)), device_id_type=MESH
        )

    @pl.loop(0, owners)
    def _(j):
        y0 = (7 * j) // 4
        parts = []
        for ref, y, rows in ((f1_ref, y0, 3), (f2_ref, y0 // 2, 2), (f3_ref, y0 // 4, 2)):
            for g in range(2):
                parts.append(ref[g, pl.ds(y, rows)].reshape(-1, LANES))
        picked = jnp.dot(
            table_ref[j], jnp.concatenate(parts, 0), preferred_element_type=jnp.float32
        )
        s_ref[:, j] = picked.reshape(groups, UNIT, LANES).astype(jnp.bfloat16)

    pl.semaphore_wait(barrier, groups - 1 + owners - 1)

    def to_group(d):
        target = lax.rem(me + d, groups)
        return pltpu.make_async_remote_copy(
            src_ref=s_ref.at[target],
            dst_ref=r1_ref.at[me],
            send_sem=a_send.at[d],
            recv_sem=a_recv.at[d],
            device_id=(target, my_pos),
            device_id_type=MESH,
        )

    def to_owner(d):
        target = lax.rem(my_pos + d, owners)
        return pltpu.make_async_remote_copy(
            src_ref=r1_ref.at[:, target],
            dst_ref=r2_ref.at[my_pos],
            send_sem=b_send.at[d],
            recv_sem=b_recv.at[d],
            device_id=(me, target),
            device_id_type=MESH,
        )

    @pl.loop(1, groups)
    def _(d):
        to_group(d).start()

    r1_ref[me] = s_ref[me]

    @pl.loop(1, groups)
    def _(d):
        to_group(d).wait()

    @pl.loop(1, owners)
    def _(d):
        to_owner(d).start()

    r2_ref[my_pos] = r1_ref[:, my_pos]

    picks, masks = flatten_tables(kept)
    picks = jnp.where(picks, 1.0, 0.0).astype(jnp.bfloat16)

    @pl.loop(1, owners)
    def _(d):
        to_owner(d).wait()

    rows = groups * owners * UNIT
    x = r2_ref[...].astype(jnp.float32).reshape(rows, LANES)
    slot = (iota((rows, LANES), 0) >> 1) & (SLOTS - 1)
    spread = jnp.concatenate([jnp.where(slot == q, x, 0.0) for q in range(SLOTS)], 1)
    gram = lax.dot_general(
        x.astype(jnp.bfloat16),
        spread.astype(jnp.bfloat16),
        (((0,), (0,)), ((), ())),
        preferred_element_type=jnp.float32,
    )

    k = iota((LANES, LANES), 0)
    eye = jnp.where(k == iota((LANES, LANES), 1), 0.01, 0.0)
    turn = k * kept
    rolled, means = [], []
    for q in range(SLOTS):
        raw = gram[:, q * LANES : (q + 1) * LANES]
        total = raw[ONES:, ONES:]
        mean = raw[ONES:, :] / total
        cov = (raw - raw[:, ONES:] * mean) / (total - 1.0) + eye
        for bit in (4, 8, 16, 32, 64):
            cov = jnp.where((turn & bit) != 0, pltpu.roll(cov, bit, 1), cov)
        rolled.append(cov.astype(jnp.bfloat16))
        means.append(mean)
    flat = jnp.dot(picks, jnp.concatenate(rolled, 1), preferred_element_type=jnp.float32)

    row, lane = iota((FLAT, LANES), 0), iota((FLAT, LANES), 1)
    used = kept * kept
    edge = used % LANES
    for q in range(SLOTS):
        packet = jnp.zeros((FLAT, LANES), jnp.float32)
        for t in range(3):
            part = flat[t * FLAT : (t + 1) * FLAT, q * LANES : (q + 1) * LANES]
            packet = packet + jnp.where(masks[t], part, 0.0)
        high = means[q].astype(jnp.bfloat16).astype(jnp.float32)
        low = pltpu.roll(jnp.broadcast_to(means[q] - high, (8, LANES)), edge, 1)[:1]
        packet = jnp.where(row == FLAT - 1, high, packet)
        packet = jnp.where((row == FLAT - 2) & (lane >= edge), low, packet)
        packet = packet.astype(jnp.bfloat16)
        if q < SLOTS - 1:
            out_ref[me, q * FLAT : (q + 1) * FLAT] = packet
        else:
            last_ref[...] = packet

    def send(chip, sems, step, device):
        part = out_ref.at[chip * 2 + core]
        copy = pltpu.make_async_remote_copy(
            src_ref=part,
            dst_ref=part,
            send_sem=sems[0].at[step],
            recv_sem=sems[1].at[step],
            device_id=device,
            device_id_type=MESH,
        )
        copy.start()
        return copy

    right = (lax.rem(z + 1, chips) * 2 + core, my_pos)
    left = (lax.rem(z + chips - 1, chips) * 2 + core, my_pos)
    partner = (z * 2 + 1 - core, my_pos)
    cw_sems, ccw_sems, pair_sems = (cw_send, cw_recv), (ccw_send, ccw_recv), (pair_send, pair_recv)
    half = chips // 2
    cw = send(z, cw_sems, 0, right)
    ccw = send(z, ccw_sems, 0, left)
    pairs = [send(z, pair_sems, 0, partner)]
    sent = [cw, ccw]
    for step in range(1, half + 1):
        came = lax.rem(z + chips - step, chips)
        cw.wait_recv()
        if step < half:
            cw = send(came, cw_sems, step, right)
            sent.append(cw)
        pairs.append(send(came, pair_sems, step, partner))
        if step < half:
            came = lax.rem(z + step, chips)
            ccw.wait_recv()
            if step < half - 1:
                ccw = send(came, ccw_sems, step, left)
                sent.append(ccw)
            pairs.append(send(came, pair_sems, half + step, partner))
    for copy in sent:
        copy.wait_send()
    for copy in pairs:
        copy.wait()


def per_device(
    section_one,
    section_two,
    section_three,
    weight_one,
    weight_two,
    weight_three,
    gain_one,
    gain_two,
    gain_three,
    bias_one,
    bias_two,
    bias_three,
    channel_index,
    valid_count,
):
    images, side = section_one.shape[:2]
    width_one, width_two = section_one.shape[3], section_two.shape[3]
    kept = channel_index.shape[0]
    groups, owners = lax.axis_size("img"), lax.axis_size("pos")
    block = side * side // owners
    scale = (lax.iota(jnp.int32, images) < valid_count[0, 0]).astype(jnp.bfloat16)
    scale = scale[:, None, None, None]
    out_one = section_out(section_one, weight_one, gain_one, bias_one) * scale
    out_two = section_out(section_two, weight_two, gain_two, bias_two) * scale
    out_three = section_out(section_three, weight_three, gain_three, bias_three) * scale
    slots = jnp.pad(channel_index, (0, LANES - kept), constant_values=-1024)
    f1 = pick_channels(out_one, 0, slots)
    f1 = jnp.where(lax.iota(jnp.int32, LANES) == ONES, scale, f1)
    f2 = pick_channels(out_two, width_one, slots)
    f3 = pick_channels(out_three, width_one + width_two, slots)
    f1 = jnp.pad(f1, ((0, 0), (0, 1), (0, 4), (0, 0)))
    f2 = jnp.pad(f2, ((0, 0), (0, 2), (0, 2), (0, 0)))
    f3 = jnp.pad(f3, ((0, 0), (0, 1), (0, 9), (0, 0)))
    table = jnp.asarray(gather_table(side, owners, groups))
    own = SLOTS - 1
    vmem = pl.BlockSpec(memory_space=pltpu.VMEM)
    dma = pltpu.SemaphoreType.DMA
    out, last = pl.pallas_call(
        functools.partial(kernel, kept),
        out_shape=(
            jax.ShapeDtypeStruct((groups, own * FLAT, LANES), jnp.bfloat16),
            jax.ShapeDtypeStruct((FLAT, LANES), jnp.bfloat16),
        ),
        in_specs=[vmem] * 4,
        out_specs=[vmem] * 2,
        scratch_shapes=[
            pltpu.VMEM((groups, owners, UNIT, LANES), jnp.bfloat16),
            pltpu.VMEM((groups, owners, UNIT, LANES), jnp.bfloat16),
            pltpu.VMEM((owners, groups, UNIT, LANES), jnp.bfloat16),
            dma((groups,)),
            dma((groups,)),
            dma((owners,)),
            dma((owners,)),
            dma((groups // 4,)),
            dma((groups // 4,)),
            dma((groups // 4,)),
            dma((groups // 4,)),
            dma((groups // 2,)),
            dma((groups // 2,)),
        ],
        compiler_params=pltpu.CompilerParams(
            collective_id=0, has_side_effects=True, vmem_limit_bytes=40 * 2**20
        ),
        cost_estimate=pl.CostEstimate(
            flops=800_000_000, bytes_accessed=4_000_000, transcendentals=0
        ),
        name="statistics",
    )(f1, f2, f3, table)
    packets = jnp.concatenate(
        [out.reshape(block - 1, FLAT * LANES), last.reshape(1, FLAT * LANES)]
    ).astype(jnp.float32)
    used = kept * kept
    covariance = packets[:, :used]
    end = (FLAT - 1) * LANES
    mean = packets[:, end : end + kept] + packets[:, used : used + kept]
    return (mean.T, covariance)


def solution(mesh):
    return jax.shard_map(
        per_device,
        mesh=mesh,
        in_specs=(P(("img", "pos"), None, None, None),) * 3
        + (P(),) * 10
        + (P("img", "pos"),),
        out_specs=(P(None, "pos"), P("pos", None)),
        check_vma=False,
    )
```

```python
import functools

import jax
import jax.numpy as jnp
import numpy as np
from jax import lax
from jax.experimental import pallas as pl
from jax.experimental.pallas import tpu as pltpu
from jax.sharding import PartitionSpec as P

MESH = pl.DeviceIdType.MESH
LANES = 128
ONES = 127
SLOTS = 4
WAVES = 2
PER_WAVE = SLOTS // WAVES
UNIT = 2 * PER_WAVE
FLAT = 80
WINDOW = 160


def section_out(images, weight, gain, bias):
    conv = lax.conv_general_dilated(
        images,
        weight,
        (1, 1),
        "SAME",
        dimension_numbers=("NHWC", "HWIO", "NHWC"),
        preferred_element_type=jnp.float32,
    )
    return jax.nn.relu(conv * gain + bias).astype(jnp.bfloat16)


def pick_channels(section, offset, slots):
    width = section.shape[3]
    table = (slots[None, :] - offset == lax.iota(jnp.int32, width)[:, None]).astype(jnp.bfloat16)
    return jnp.einsum(
        "ihwc,ck->ihwk", section, table, preferred_element_type=jnp.float32
    ).astype(jnp.bfloat16)


def gather_index(side, blocks, sharers):
    block = side * side // blocks
    own = block // sharers
    rows = sharers * UNIT
    index = np.full((WAVES * rows, LANES), -1, np.int32)
    for j in range(blocks):
        y0 = j * block // side
        for place in range(sharers):
            half, pair = divmod(place, sharers // 2)
            i = pair * 2 + (j + half) % 2
            for q in range(SLOTS):
                wave, part = divmod(q, PER_WAVE)
                position = j * block + (i * own + q if q < own else block - 1)
                y, x = divmod(position, side)
                columns = (
                    (y - y0) * 32 + x,
                    96 + (y // 2 - y0 // 2) * 16 + x // 2,
                    128 + (y // 4 - y0 // 4) * 16 + x // 4,
                )
                for g in range(2):
                    row = wave * rows + place * UNIT + g * PER_WAVE + part
                    index[row, j * 3 : j * 3 + 3] = columns
    return index


def iota(shape, dim):
    return lax.broadcasted_iota(jnp.int32, shape, dim)


def flatten_tables(kept):
    f = iota((FLAT, LANES), 0) * LANES
    k = iota((FLAT, LANES), 1)
    picks, masks = [], []
    start = jnp.floor((f.astype(jnp.float32) + 0.5) * (1.0 / kept))
    rest = f - start.astype(jnp.int32) * kept + k
    for t in range(3):
        picks.append(((k - t) * kept <= f) & (f < (k - t + 1) * kept))
        masks.append((rest >= t * kept) & (rest < (t + 1) * kept))
    return jnp.concatenate(picks, 0), masks


def packets(kept, gram, picks, masks, q):
    raw = gram[:, q * LANES : (q + 1) * LANES]
    k = iota((LANES, LANES), 0)
    eye = jnp.where(k == iota((LANES, LANES), 1), 0.01, 0.0)
    total = raw[ONES:, ONES:]
    mean = raw[ONES:, :] / total
    cov = (raw - raw[:, ONES:] * mean) / (total - 1.0) + eye
    for bit in (4, 8, 16, 32, 64):
        cov = jnp.where(((k * kept) & bit) != 0, pltpu.roll(cov, bit, 1), cov)
    flat = jnp.dot(picks, cov.astype(jnp.bfloat16), preferred_element_type=jnp.float32)
    packet = jnp.zeros((FLAT, LANES), jnp.float32)
    for t in range(3):
        packet = packet + jnp.where(masks[t], flat[t * FLAT : (t + 1) * FLAT], 0.0)
    row, lane = iota((FLAT, LANES), 0), iota((FLAT, LANES), 1)
    edge = kept * kept % LANES
    high = mean.astype(jnp.bfloat16).astype(jnp.float32)
    low = pltpu.roll(jnp.broadcast_to(mean - high, (8, LANES)), edge, 1)[:1]
    packet = jnp.where(row == FLAT - 1, high, packet)
    packet = jnp.where((row == FLAT - 2) & (lane >= edge), low, packet)
    return packet.astype(jnp.bfloat16)


def kernel(
    kept,
    f1_ref,
    f2_ref,
    f3_ref,
    index_hbm,
    out_ref,
    last_ref,
    index_ref,
    fetch_sem,
    s1_ref,
    s2_ref,
    r1_ref,
    r2_ref,
    x_ref,
    a_send,
    a_recv,
    b_send,
    b_recv,
    c_send,
    d_send,
    x_recv,
    z_send,
    z_recv,
    pair_send,
    pair_recv,
):
    groups, owners = r1_ref.shape[1], r2_ref.shape[1]
    chips = groups // 2
    me = lax.axis_index("img")
    pos = lax.axis_index("pos")
    z, core = me // 2, me % 2
    odd = (me + pos) % 2

    fetch = pltpu.make_async_copy(index_hbm, index_ref, fetch_sem)
    fetch.start()
    barrier = pltpu.get_barrier_semaphore()

    @pl.loop(1, groups)
    def _(d):
        pl.semaphore_signal(
            barrier, inc=1, device_id=(lax.rem(me + d, groups), pos), device_id_type=MESH
        )

    @pl.loop(1, owners)
    def _(d):
        pl.semaphore_signal(
            barrier, inc=1, device_id=(me, lax.rem(pos + d, owners)), device_id_type=MESH
        )

    fetch.wait()
    rows = WAVES * groups * UNIT
    column = iota((rows, WINDOW), 1)
    second = (iota((rows, LANES), 0) & PER_WAVE) != 0
    for j in range(owners):
        y0 = (7 * j) // 4
        halves = []
        for g in range(2):
            parts = []
            for ref, y, count in ((f1_ref, y0, 3), (f2_ref, y0 // 2, 2), (f3_ref, y0 // 4, 2)):
                parts.append(ref[g, y : y + count].reshape(-1, LANES))
            halves.append(jnp.concatenate(parts, 0))
        table = column == index_ref[:, 3 * j : 3 * j + 1]
        for t in (1, 2):
            table = table | (column == index_ref[:, 3 * j + t : 3 * j + t + 1])
        table = jnp.where(table, 1.0, 0.0).astype(jnp.bfloat16)
        both = jnp.dot(table, jnp.concatenate(halves, 1), preferred_element_type=jnp.float32)
        picked = jnp.where(second, both[:, LANES:], both[:, :LANES])
        picked = picked.reshape(WAVES, 2, groups // 2, UNIT, LANES).astype(jnp.bfloat16)
        for wave in range(WAVES):
            s1_ref[wave, :, j % 2, j // 2] = picked[wave, 0]
            s2_ref[wave, j] = picked[wave, 1]

    pl.semaphore_wait(barrier, groups - 1 + owners - 1)

    def remote(src, dst, send_sem, recv_sem, device):
        return pltpu.make_async_remote_copy(
            src_ref=src,
            dst_ref=dst,
            send_sem=send_sem,
            recv_sem=recv_sem,
            device_id=device,
            device_id_type=MESH,
        )

    def to_group(wave, d):
        to = lax.rem(me + d, groups)
        source = s1_ref.at[wave, to // 2, to % 2]
        sems = a_send.at[wave, d], a_recv.at[wave, d]
        return remote(source, r1_ref.at[wave, me], *sems, (to, pos))

    def to_owner(wave, d):
        to = lax.rem(pos + d, owners)
        sems = b_send.at[wave, d], b_recv.at[wave, d]
        return remote(s2_ref.at[wave, to], r2_ref.at[wave, pos], *sems, (me, to))

    def on_to_owner(wave, n):
        to = lax.rem(pos // 2 + n, owners // 2)
        sems = c_send.at[wave, n], x_recv.at[wave, pos]
        return remote(r1_ref.at[wave, :, to], x_ref.at[wave, pos], *sems, (me, 2 * to + core))

    def on_to_group(wave, n):
        to = lax.rem(z + n, chips)
        sems = d_send.at[wave, n], x_recv.at[wave, me]
        device = (2 * to + 1 - pos % 2, pos)
        return remote(r2_ref.at[wave, :, to], x_ref.at[wave, me], *sems, device)

    def far_first(n, count):
        return count // 2 + ((n + 1) // 2) * (1 - 2 * (n % 2))

    for wave in range(WAVES):

        @pl.loop(0, groups - 1)
        def _(n, wave=wave):
            to_group(wave, far_first(n, groups)).start()
            to_owner(wave, far_first(n, owners)).start()

    for wave in range(WAVES):
        r1_ref[wave, me] = s1_ref[wave, z, core]
        r2_ref[wave, pos] = s2_ref[wave, pos]
    tables = flatten_tables(kept)
    masks = tables[1]
    picks = jnp.where(tables[0], 1.0, 0.0).astype(jnp.bfloat16)

    for wave in range(WAVES):

        @pl.loop(1, owners)
        def _(d, wave=wave):
            to_owner(wave, d).wait()

        @pl.loop(odd, chips)
        def _(n, wave=wave):
            on_to_group(wave, n).start()

        @pl.loop(1, groups)
        def _(d, wave=wave):
            to_group(wave, d).wait()

        @pl.loop(1 - odd, owners // 2)
        def _(n, wave=wave):
            on_to_owner(wave, n).start()

    @pl.when(odd == 0)
    def _():
        for wave in range(WAVES):
            x_ref[wave, pos] = r1_ref[wave, :, pos // 2]

    @pl.when(odd == 1)
    def _():
        for wave in range(WAVES):
            x_ref[wave, me] = r2_ref[wave, :, z]

    mine = jnp.where(odd == 0, pos, me)

    def wave_gram(wave):
        @pl.loop(1, owners)
        def _(d):
            source = lax.rem(mine + d, owners)
            part = x_ref.at[wave, source]
            pltpu.make_async_copy(part, part, x_recv.at[wave, source]).wait()

        units = groups * owners
        x = x_ref[wave].astype(jnp.float32).reshape(units // 2, 2, UNIT, LANES)
        x = jnp.concatenate([x[:, 0], x[:, 1]], 1).reshape(units * UNIT, LANES)
        slot = iota((units * UNIT, LANES), 0) & (PER_WAVE - 1)
        spread = jnp.concatenate([jnp.where(slot == q, x, 0.0) for q in range(PER_WAVE)], 1)
        return lax.dot_general(
            x.astype(jnp.bfloat16),
            spread.astype(jnp.bfloat16),
            (((0,), (0,)), ((), ())),
            preferred_element_type=jnp.float32,
        )

    def device_at(distance):
        return (lax.rem(z + distance, chips) * 2 + core, pos)

    for q in range(SLOTS):
        if q % PER_WAVE == 0:
            gram = wave_gram(q // PER_WAVE)
        if q == SLOTS - 1:
            break
        rows = pl.ds(q * FLAT, FLAT)
        out_ref[me, rows] = packets(kept, gram, picks, masks, q % PER_WAVE)
        part = out_ref.at[me, rows]
        for distance in (4, 3, 5, 2, 6, 1, 7):
            sems = z_send.at[distance], z_recv.at[distance]
            remote(part, part, *sems, device_at(distance)).start()
    partner = (z * 2 + 1 - core, pos)

    def share(distance):
        part = out_ref.at[lax.rem(z + chips - distance, chips) * 2 + core]
        return remote(part, part, pair_send.at[distance], pair_recv.at[distance], partner)

    share(0).start()
    last_ref[...] = packets(kept, gram, picks, masks, PER_WAVE - 1)
    whole = out_ref.at[me]
    for distance in (1, 7, 2, 6, 3, 5, 4):
        sems = z_send.at[distance], z_recv.at[distance]
        remote(whole, whole, *sems, device_at(distance)).wait_recv()
        share(distance).start()
    for distance in range(1, chips):
        sems = z_send.at[distance], z_recv.at[distance]
        remote(whole, whole, *sems, device_at(distance)).wait_send()

    for wave in range(WAVES):

        @pl.loop(odd, chips)
        def _(n, wave=wave):
            on_to_group(wave, n).wait_send()

        @pl.loop(1 - odd, owners // 2)
        def _(n, wave=wave):
            on_to_owner(wave, n).wait_send()

    for distance in range(chips):
        share(distance).wait()


def per_device(
    section_one,
    section_two,
    section_three,
    weight_one,
    weight_two,
    weight_three,
    gain_one,
    gain_two,
    gain_three,
    bias_one,
    bias_two,
    bias_three,
    channel_index,
    valid_count,
):
    images, side = section_one.shape[:2]
    width_one, width_two = section_one.shape[3], section_two.shape[3]
    kept = channel_index.shape[0]
    groups, owners = lax.axis_size("img"), lax.axis_size("pos")
    block = side * side // owners
    scale = (lax.iota(jnp.int32, images) < valid_count[0, 0]).astype(jnp.bfloat16)
    scale = scale[:, None, None, None]
    out_one = section_out(section_one, weight_one, gain_one, bias_one) * scale
    out_two = section_out(section_two, weight_two, gain_two, bias_two) * scale
    out_three = section_out(section_three, weight_three, gain_three, bias_three) * scale
    slots = jnp.pad(channel_index, (0, LANES - kept), constant_values=-1024)
    f1 = pick_channels(out_one, 0, slots)
    f1 = jnp.where(lax.iota(jnp.int32, LANES) == ONES, scale, f1)
    f2 = pick_channels(out_two, width_one, slots)
    f3 = pick_channels(out_three, width_one + width_two, slots)
    f1 = jnp.pad(f1, ((0, 0), (0, 1), (0, 4), (0, 0)))
    f2 = jnp.pad(f2, ((0, 0), (0, 2), (0, 2), (0, 0)))
    f3 = jnp.pad(f3, ((0, 0), (0, 1), (0, 9), (0, 0)))
    index = jnp.asarray(gather_index(side, owners, groups))
    own = SLOTS - 1
    vmem = pl.BlockSpec(memory_space=pltpu.VMEM)
    dma = pltpu.SemaphoreType.DMA
    out, last = pl.pallas_call(
        functools.partial(kernel, kept),
        out_shape=(
            jax.ShapeDtypeStruct((groups, own * FLAT, LANES), jnp.bfloat16),
            jax.ShapeDtypeStruct((FLAT, LANES), jnp.bfloat16),
        ),
        in_specs=[vmem] * 3 + [pl.BlockSpec(memory_space=pl.ANY)],
        out_specs=[vmem] * 2,
        scratch_shapes=[
            pltpu.VMEM(index.shape, jnp.int32),
            dma(()),
            pltpu.VMEM((WAVES, groups // 2, 2, owners // 2, UNIT, LANES), jnp.bfloat16),
            pltpu.VMEM((WAVES, owners, groups // 2, UNIT, LANES), jnp.bfloat16),
            pltpu.VMEM((WAVES, groups, owners // 2, UNIT, LANES), jnp.bfloat16),
            pltpu.VMEM((WAVES, owners, groups // 2, UNIT, LANES), jnp.bfloat16),
            pltpu.VMEM((WAVES, owners, groups, UNIT, LANES), jnp.bfloat16),
            dma((WAVES, groups)),
            dma((WAVES, groups)),
            dma((WAVES, owners)),
            dma((WAVES, owners)),
            dma((WAVES, owners // 2)),
            dma((WAVES, groups // 2)),
            dma((WAVES, owners)),
            dma((groups // 2,)),
            dma((groups // 2,)),
            dma((groups // 2,)),
            dma((groups // 2,)),
        ],
        compiler_params=pltpu.CompilerParams(
            collective_id=0, has_side_effects=True, vmem_limit_bytes=40 * 2**20
        ),
        cost_estimate=pl.CostEstimate(
            flops=800_000_000, bytes_accessed=4_000_000, transcendentals=0
        ),
        name="statistics",
    )(f1, f2, f3, index)
    packets = jnp.concatenate(
        [out.reshape(block - 1, FLAT * LANES), last.reshape(1, FLAT * LANES)]
    ).astype(jnp.float32)
    used = kept * kept
    covariance = packets[:, :used]
    end = (FLAT - 1) * LANES
    mean = packets[:, end : end + kept] + packets[:, used : used + kept]
    return (mean.T, covariance)


def solution(mesh):
    return jax.shard_map(
        per_device,
        mesh=mesh,
        in_specs=(P(("img", "pos"), None, None, None),) * 3
        + (P(),) * 10
        + (P("img", "pos"),),
        out_specs=(P(None, "pos"), P("pos", None)),
        check_vma=False,
    )
```

```python
import functools

import jax
import jax.numpy as jnp
import numpy as np
from jax import lax
from jax.experimental import pallas as pl
from jax.experimental.pallas import tpu as pltpu
from jax.sharding import PartitionSpec as P

MESH = pl.DeviceIdType.MESH
LANES = 128
ONES = 127
SLOTS = 4
WAVES = 2
PER_WAVE = SLOTS // WAVES
UNIT = 2 * PER_WAVE
FLAT = 80
WINDOW = 160
WHOLE = ((0, 2 * FLAT), (2 * FLAT, FLAT))
LOWER = ((0, FLAT), (2 * FLAT, 32))
UPPER = ((FLAT, FLAT), (2 * FLAT + 32, FLAT - 32))


def section_out(images, weight, gain, bias):
    conv = lax.conv_general_dilated(
        images,
        weight,
        (1, 1),
        "SAME",
        dimension_numbers=("NHWC", "HWIO", "NHWC"),
        preferred_element_type=jnp.float32,
    )
    return jax.nn.relu(conv * gain + bias).astype(jnp.bfloat16)


def pick_channels(section, offset, slots):
    width = section.shape[3]
    table = (slots[None, :] - offset == lax.iota(jnp.int32, width)[:, None]).astype(jnp.bfloat16)
    return jnp.einsum(
        "ihwc,ck->ihwk", section, table, preferred_element_type=jnp.float32
    ).astype(jnp.bfloat16)


def gather_index(side, blocks, sharers):
    block = side * side // blocks
    own = block // sharers
    rows = sharers * UNIT
    index = np.full((WAVES * rows, LANES), -1, np.int32)
    for j in range(blocks):
        y0 = j * block // side
        for place in range(sharers):
            half, pair = divmod(place, sharers // 2)
            i = pair * 2 + (j + half) % 2
            for q in range(SLOTS):
                wave, part = divmod(q, PER_WAVE)
                position = j * block + (i * own + q if q < own else block - 1)
                y, x = divmod(position, side)
                columns = (
                    (y - y0) * 32 + x,
                    96 + (y // 2 - y0 // 2) * 16 + x // 2,
                    128 + (y // 4 - y0 // 4) * 16 + x // 4,
                )
                for g in range(2):
                    row = wave * rows + place * UNIT + g * PER_WAVE + part
                    index[row, j * 3 : j * 3 + 3] = columns
    return index


def iota(shape, dim):
    return lax.broadcasted_iota(jnp.int32, shape, dim)


def flatten_tables(kept):
    f = iota((FLAT, LANES), 0) * LANES
    k = iota((FLAT, LANES), 1)
    picks, masks = [], []
    start = jnp.floor((f.astype(jnp.float32) + 0.5) * (1.0 / kept))
    rest = f - start.astype(jnp.int32) * kept + k
    for t in range(3):
        picks.append(((k - t) * kept <= f) & (f < (k - t + 1) * kept))
        masks.append((rest >= t * kept) & (rest < (t + 1) * kept))
    return jnp.concatenate(picks, 0), masks


def packets(kept, gram, picks, masks, q):
    raw = gram[:, q * LANES : (q + 1) * LANES]
    k = iota((LANES, LANES), 0)
    eye = jnp.where(k == iota((LANES, LANES), 1), 0.01, 0.0)
    total = raw[ONES:, ONES:]
    mean = raw[ONES:, :] / total
    cov = (raw - raw[:, ONES:] * mean) / (total - 1.0) + eye
    for bit in (4, 8, 16, 32, 64):
        cov = jnp.where(((k * kept) & bit) != 0, pltpu.roll(cov, bit, 1), cov)
    flat = jnp.dot(picks, cov.astype(jnp.bfloat16), preferred_element_type=jnp.float32)
    packet = jnp.zeros((FLAT, LANES), jnp.float32)
    for t in range(3):
        packet = packet + jnp.where(masks[t], flat[t * FLAT : (t + 1) * FLAT], 0.0)
    row, lane = iota((FLAT, LANES), 0), iota((FLAT, LANES), 1)
    edge = kept * kept % LANES
    high = mean.astype(jnp.bfloat16).astype(jnp.float32)
    low = pltpu.roll(jnp.broadcast_to(mean - high, (8, LANES)), edge, 1)[:1]
    packet = jnp.where(row == FLAT - 1, high, packet)
    packet = jnp.where((row == FLAT - 2) & (lane >= edge), low, packet)
    return packet.astype(jnp.bfloat16)


def kernel(
    kept,
    f1_ref,
    f2_ref,
    f3_ref,
    index_hbm,
    out_ref,
    last_ref,
    index_ref,
    index_sem,
    s1_ref,
    s2_ref,
    r1_ref,
    r2_ref,
    x_ref,
    a_send,
    a_recv,
    b_send,
    b_recv,
    c_send,
    d_send,
    x_recv,
    z_send,
    z_recv,
    pair_send,
    pair_recv,
):
    groups, owners = r1_ref.shape[1], r2_ref.shape[1]
    chips = groups // 2
    me = lax.axis_index("img")
    pos = lax.axis_index("pos")
    z, core = me // 2, me % 2
    odd = (me + pos) % 2

    fetch = pltpu.make_async_copy(index_hbm, index_ref, index_sem)
    fetch.start()
    barrier = pltpu.get_barrier_semaphore()

    @pl.loop(1, groups)
    def _(d):
        pl.semaphore_signal(
            barrier, inc=1, device_id=(lax.rem(me + d, groups), pos), device_id_type=MESH
        )

    @pl.loop(1, owners)
    def _(d):
        pl.semaphore_signal(
            barrier, inc=1, device_id=(me, lax.rem(pos + d, owners)), device_id_type=MESH
        )

    rows = groups * UNIT
    second = (iota((rows, LANES), 0) & PER_WAVE) != 0

    column = iota((rows, WINDOW), 1)
    fetch.wait()

    def gather(wave):
        for j in range(owners):
            table = False
            for t in range(3):
                at = index_ref[wave * rows : (wave + 1) * rows, 3 * j + t : 3 * j + t + 1]
                table = table | (column == at)
            y0 = (7 * j) // 4
            halves = []
            for g in range(2):
                parts = []
                for ref, y, count in ((f1_ref, y0, 3), (f2_ref, y0 // 2, 2), (f3_ref, y0 // 4, 2)):
                    parts.append(ref[g, y : y + count].reshape(-1, LANES))
                halves.append(jnp.concatenate(parts, 0))
            both = jnp.dot(
                jnp.where(table, 1.0, 0.0).astype(jnp.bfloat16),
                jnp.concatenate(halves, 1),
                preferred_element_type=jnp.float32,
            )
            picked = jnp.where(second, both[:, LANES:], both[:, :LANES])
            picked = picked.reshape(2, groups // 2, UNIT, LANES).astype(jnp.bfloat16)
            s1_ref[wave, :, j % 2, j // 2] = picked[0]
            s2_ref[wave, j] = picked[1]

    def remote(src, dst, send_sem, recv_sem, device):
        return pltpu.make_async_remote_copy(
            src_ref=src,
            dst_ref=dst,
            send_sem=send_sem,
            recv_sem=recv_sem,
            device_id=device,
            device_id_type=MESH,
        )

    def to_group(wave, d):
        to = lax.rem(me + d, groups)
        source = s1_ref.at[wave, to // 2, to % 2]
        sems = a_send.at[wave, d], a_recv.at[wave, d]
        return remote(source, r1_ref.at[wave, me], *sems, (to, pos))

    def to_owner(wave, d):
        to = lax.rem(pos + d, owners)
        sems = b_send.at[wave, d], b_recv.at[wave, d]
        return remote(s2_ref.at[wave, to], r2_ref.at[wave, pos], *sems, (me, to))

    def on_to_owner(wave, n):
        to = lax.rem(pos // 2 + n, owners // 2)
        sems = c_send.at[wave, n], x_recv.at[wave, pos]
        return remote(r1_ref.at[wave, :, to], x_ref.at[wave, pos], *sems, (me, 2 * to + core))

    def on_to_group(wave, n):
        to = lax.rem(z + n, chips)
        sems = d_send.at[wave, n], x_recv.at[wave, me]
        device = (2 * to + 1 - pos % 2, pos)
        return remote(r2_ref.at[wave, :, to], x_ref.at[wave, me], *sems, device)

    def far_first(n, count):
        return count // 2 + ((n + 1) // 2) * (1 - 2 * (n % 2))

    for wave in range(WAVES):
        gather(wave)
        if wave == 0:
            pl.semaphore_wait(barrier, groups - 1 + owners - 1)

        @pl.loop(0, groups - 1)
        def _(n, wave=wave):
            to_group(wave, far_first(n, groups)).start()

        @pl.loop(0, owners - 1)
        def _(n, wave=wave):
            to_owner(wave, far_first(n, owners)).start()

    for wave in range(WAVES):
        r1_ref[wave, me] = s1_ref[wave, z, core]
        r2_ref[wave, pos] = s2_ref[wave, pos]
    tables = flatten_tables(kept)
    masks = tables[1]
    picks = jnp.where(tables[0], 1.0, 0.0).astype(jnp.bfloat16)

    for wave in range(WAVES):

        @pl.loop(1, owners)
        def _(d, wave=wave):
            to_owner(wave, d).wait()

        @pl.loop(odd, chips)
        def _(n, wave=wave):
            on_to_group(wave, n).start()

        @pl.loop(1, groups)
        def _(d, wave=wave):
            to_group(wave, d).wait()

        @pl.loop(1 - odd, owners // 2)
        def _(n, wave=wave):
            on_to_owner(wave, n).start()

    @pl.when(odd == 0)
    def _():
        for wave in range(WAVES):
            x_ref[wave, pos] = r1_ref[wave, :, pos // 2]

    @pl.when(odd == 1)
    def _():
        for wave in range(WAVES):
            x_ref[wave, me] = r2_ref[wave, :, z]

    mine = jnp.where(odd == 0, pos, me)

    def wave_gram(wave):
        @pl.loop(1, owners)
        def _(d):
            source = lax.rem(mine + d, owners)
            part = x_ref.at[wave, source]
            pltpu.make_async_copy(part, part, x_recv.at[wave, source]).wait()

        units = groups * owners
        x = x_ref[wave].astype(jnp.float32).reshape(units // 2, 2, UNIT, LANES)
        x = jnp.concatenate([x[:, 0], x[:, 1]], 1).reshape(units * UNIT, LANES)
        slot = iota((units * UNIT, LANES), 0) & (PER_WAVE - 1)
        spread = jnp.concatenate([jnp.where(slot == q, x, 0.0) for q in range(PER_WAVE)], 1)
        return lax.dot_general(
            x.astype(jnp.bfloat16),
            spread.astype(jnp.bfloat16),
            (((0,), (0,)), ((), ())),
            preferred_element_type=jnp.float32,
        )

    def slot_at(distance):
        return lax.rem(z + chips - distance, chips) * 2 + core

    def share(rows, origin, target, sems, send, came):
        part = out_ref.at[slot_at(origin), pl.ds(*rows)]
        device = (lax.rem(z + target, chips) * 2 + core, pos)
        return remote(part, part, z_send.at[sems, send], z_recv.at[sems, came], device)

    def pair(wave, origin):
        part = out_ref.at[slot_at(origin), pl.ds(*WHOLE[wave])]
        sems = pair_send.at[wave, origin], pair_recv.at[wave, origin]
        return remote(part, part, *sems, (z * 2 + 1 - core, pos))

    sent = []

    def begin(wave):
        for target in (2, 6, 1, 7):
            sent.append(share(WHOLE[wave], 0, target, wave, target, target))
            sent[-1].start()

    def arrive(wave, origin):
        if origin == 4:
            share(LOWER[wave], 4, 1, wave, 0, 4).wait_recv()
            share(UPPER[wave], 4, 1, wave, 0, 0).wait_recv()
        else:
            share(WHOLE[wave], origin, 1, wave, 0, origin).wait_recv()
        if origin == 2:
            sent.append(share(LOWER[wave], 2, 2, wave, 4, 4))
            sent.append(share(WHOLE[wave], 2, 1, wave, 3, 3))
        elif origin == 6:
            sent.append(share(UPPER[wave], 6, 6, wave, 0, 0))
            sent.append(share(WHOLE[wave], 6, 7, wave, 5, 5))
        if origin in (2, 6):
            sent[-2].start()
            sent[-1].start()
        pair(wave, origin).start()

    for q in range(SLOTS - 1):
        if q % PER_WAVE == 0:
            gram = wave_gram(q // PER_WAVE)
        rows = pl.ds(q * FLAT, FLAT)
        out_ref[me, rows] = packets(kept, gram, picks, masks, q % PER_WAVE)
        if q == PER_WAVE - 1:
            begin(0)
            pair(0, 0).start()
    begin(1)
    pair(1, 0).start()
    last_ref[...] = packets(kept, gram, picks, masks, PER_WAVE - 1)
    for wave in range(WAVES):
        for origin in (2, 6, 1, 7):
            arrive(wave, origin)
    for wave in range(WAVES):
        for origin in (3, 5, 4):
            arrive(wave, origin)
    for copy in sent:
        copy.wait_send()

    for wave in range(WAVES):

        @pl.loop(odd, chips)
        def _(n, wave=wave):
            on_to_group(wave, n).wait_send()

        @pl.loop(1 - odd, owners // 2)
        def _(n, wave=wave):
            on_to_owner(wave, n).wait_send()

    for wave in range(WAVES):
        for origin in range(chips):
            pair(wave, origin).wait()


def per_device(
    section_one,
    section_two,
    section_three,
    weight_one,
    weight_two,
    weight_three,
    gain_one,
    gain_two,
    gain_three,
    bias_one,
    bias_two,
    bias_three,
    channel_index,
    valid_count,
):
    images, side = section_one.shape[:2]
    width_one, width_two = section_one.shape[3], section_two.shape[3]
    kept = channel_index.shape[0]
    groups, owners = lax.axis_size("img"), lax.axis_size("pos")
    block = side * side // owners
    scale = (lax.iota(jnp.int32, images) < valid_count[0, 0]).astype(jnp.bfloat16)
    scale = scale[:, None, None, None]
    out_one = section_out(section_one, weight_one, gain_one, bias_one) * scale
    out_two = section_out(section_two, weight_two, gain_two, bias_two) * scale
    out_three = section_out(section_three, weight_three, gain_three, bias_three) * scale
    slots = jnp.pad(channel_index, (0, LANES - kept), constant_values=-1024)
    f1 = pick_channels(out_one, 0, slots)
    f1 = jnp.where(lax.iota(jnp.int32, LANES) == ONES, scale, f1)
    f2 = pick_channels(out_two, width_one, slots)
    f3 = pick_channels(out_three, width_one + width_two, slots)
    f1 = jnp.pad(f1, ((0, 0), (0, 1), (0, 4), (0, 0)))
    f2 = jnp.pad(f2, ((0, 0), (0, 2), (0, 2), (0, 0)))
    f3 = jnp.pad(f3, ((0, 0), (0, 1), (0, 9), (0, 0)))
    index = jnp.asarray(gather_index(side, owners, groups))
    own = SLOTS - 1
    vmem = pl.BlockSpec(memory_space=pltpu.VMEM)
    dma = pltpu.SemaphoreType.DMA
    out, last = pl.pallas_call(
        functools.partial(kernel, kept),
        out_shape=(
            jax.ShapeDtypeStruct((groups, own * FLAT, LANES), jnp.bfloat16),
            jax.ShapeDtypeStruct((FLAT, LANES), jnp.bfloat16),
        ),
        in_specs=[vmem] * 3 + [pl.BlockSpec(memory_space=pltpu.HBM)],
        out_specs=[vmem] * 2,
        scratch_shapes=[
            pltpu.VMEM(index.shape, jnp.int32),
            dma(()),
            pltpu.VMEM((WAVES, groups // 2, 2, owners // 2, UNIT, LANES), jnp.bfloat16),
            pltpu.VMEM((WAVES, owners, groups // 2, UNIT, LANES), jnp.bfloat16),
            pltpu.VMEM((WAVES, groups, owners // 2, UNIT, LANES), jnp.bfloat16),
            pltpu.VMEM((WAVES, owners, groups // 2, UNIT, LANES), jnp.bfloat16),
            pltpu.VMEM((WAVES, owners, groups, UNIT, LANES), jnp.bfloat16),
            dma((WAVES, groups)),
            dma((WAVES, groups)),
            dma((WAVES, owners)),
            dma((WAVES, owners)),
            dma((WAVES, owners // 2)),
            dma((WAVES, groups // 2)),
            dma((WAVES, owners)),
            dma((WAVES, groups // 2)),
            dma((WAVES, groups // 2)),
            dma((WAVES, groups // 2)),
            dma((WAVES, groups // 2)),
        ],
        compiler_params=pltpu.CompilerParams(
            collective_id=0, has_side_effects=True, vmem_limit_bytes=40 * 2**20
        ),
        cost_estimate=pl.CostEstimate(
            flops=800_000_000, bytes_accessed=4_000_000, transcendentals=0
        ),
        name="statistics",
    )(f1, f2, f3, index)
    packets = jnp.concatenate(
        [out.reshape(block - 1, FLAT * LANES), last.reshape(1, FLAT * LANES)]
    ).astype(jnp.float32)
    used = kept * kept
    covariance = packets[:, :used]
    end = (FLAT - 1) * LANES
    mean = packets[:, end : end + kept] + packets[:, used : used + kept]
    return (mean.T, covariance)


def solution(mesh):
    return jax.shard_map(
        per_device,
        mesh=mesh,
        in_specs=(P(("img", "pos"), None, None, None),) * 3
        + (P(),) * 10
        + (P("img", "pos"),),
        out_specs=(P(None, "pos"), P("pos", None)),
        check_vma=False,
    )
```

```python
import functools

import jax
import jax.numpy as jnp
import numpy as np
from jax import lax
from jax.experimental import pallas as pl
from jax.experimental.pallas import tpu as pltpu
from jax.sharding import PartitionSpec as P

MESH = pl.DeviceIdType.MESH
LANES = 128
ONES = 127
SLOTS = 4
WAVES = 2
PER_WAVE = SLOTS // WAVES
UNIT = 2 * PER_WAVE
FLAT = 80
WINDOW = 160
WHOLE = ((0, 2 * FLAT), (2 * FLAT, FLAT))
LOWER = ((0, FLAT), (2 * FLAT, 32))
UPPER = ((FLAT, FLAT), (2 * FLAT + 32, FLAT - 32))


def section_out(images, weight, gain, bias):
    conv = lax.conv_general_dilated(
        images,
        weight,
        (1, 1),
        "SAME",
        dimension_numbers=("NHWC", "HWIO", "NHWC"),
        preferred_element_type=jnp.float32,
    )
    return jax.nn.relu(conv * gain + bias).astype(jnp.bfloat16)


def pick_channels(section, offset, slots):
    width = section.shape[3]
    table = (slots[None, :] - offset == lax.iota(jnp.int32, width)[:, None]).astype(jnp.bfloat16)
    return jnp.einsum(
        "ihwc,ck->ihwk", section, table, preferred_element_type=jnp.float32
    ).astype(jnp.bfloat16)


def gather_index(side, blocks, sharers):
    block = side * side // blocks
    own = block // sharers
    rows = sharers * UNIT
    index = np.full((WAVES * rows, LANES), -1, np.int32)
    for j in range(blocks):
        y0 = j * block // side
        for place in range(sharers):
            half, pair = divmod(place, sharers // 2)
            i = pair * 2 + (j + half) % 2
            for q in range(SLOTS):
                wave, part = divmod(q, PER_WAVE)
                position = j * block + (i * own + q if q < own else block - 1)
                y, x = divmod(position, side)
                columns = (
                    (y - y0) * 32 + x,
                    96 + (y // 2 - y0 // 2) * 16 + x // 2,
                    128 + (y // 4 - y0 // 4) * 16 + x // 4,
                )
                for g in range(2):
                    row = wave * rows + place * UNIT + g * PER_WAVE + part
                    index[row, j * 3 : j * 3 + 3] = columns
    return index


def iota(shape, dim):
    return lax.broadcasted_iota(jnp.int32, shape, dim)


def flatten_tables(kept):
    f = iota((FLAT, LANES), 0) * LANES
    k = iota((FLAT, LANES), 1)
    picks, masks = [], []
    start = jnp.floor((f.astype(jnp.float32) + 0.5) * (1.0 / kept))
    rest = f - start.astype(jnp.int32) * kept + k
    for t in range(3):
        picks.append(((k - t) * kept <= f) & (f < (k - t + 1) * kept))
        masks.append((rest >= t * kept) & (rest < (t + 1) * kept))
    return jnp.concatenate(picks, 0), masks


def packets(kept, gram, picks, masks, q):
    raw = gram[:, q * LANES : (q + 1) * LANES]
    k = iota((LANES, LANES), 0)
    eye = jnp.where(k == iota((LANES, LANES), 1), 0.01, 0.0)
    total = raw[ONES:, ONES:]
    mean = raw[ONES:, :] / total
    cov = (raw - raw[:, ONES:] * mean) / (total - 1.0) + eye
    for bit in (4, 8, 16, 32, 64):
        cov = jnp.where(((k * kept) & bit) != 0, pltpu.roll(cov, bit, 1), cov)
    flat = jnp.dot(picks, cov.astype(jnp.bfloat16), preferred_element_type=jnp.float32)
    packet = jnp.zeros((FLAT, LANES), jnp.float32)
    for t in range(3):
        packet = packet + jnp.where(masks[t], flat[t * FLAT : (t + 1) * FLAT], 0.0)
    row, lane = iota((FLAT, LANES), 0), iota((FLAT, LANES), 1)
    edge = kept * kept % LANES
    high = mean.astype(jnp.bfloat16).astype(jnp.float32)
    low = pltpu.roll(jnp.broadcast_to(mean - high, (8, LANES)), edge, 1)[:1]
    packet = jnp.where(row == FLAT - 1, high, packet)
    packet = jnp.where((row == FLAT - 2) & (lane >= edge), low, packet)
    return packet.astype(jnp.bfloat16)


def kernel(
    kept,
    f1_ref,
    f2_ref,
    f3_ref,
    index_hbm,
    out_ref,
    last_ref,
    index_ref,
    index_sem,
    s1_ref,
    s2_ref,
    r1_ref,
    r2_ref,
    x_ref,
    a_send,
    a_recv,
    b_send,
    b_recv,
    x_send,
    x_recv,
    z_send,
    z_recv,
    pair_send,
    pair_recv,
):
    groups, owners = r1_ref.shape[1], r2_ref.shape[1]
    chips = groups // 2
    me = lax.axis_index("img")
    pos = lax.axis_index("pos")
    z, core = me // 2, me % 2
    odd = (me + pos) % 2

    fetch = pltpu.make_async_copy(index_hbm, index_ref, index_sem)
    fetch.start()
    barrier = pltpu.get_barrier_semaphore()

    @pl.loop(1, groups)
    def _(d):
        pl.semaphore_signal(
            barrier, inc=1, device_id=(lax.rem(me + d, groups), pos), device_id_type=MESH
        )

    @pl.loop(1, owners)
    def _(d):
        pl.semaphore_signal(
            barrier, inc=1, device_id=(me, lax.rem(pos + d, owners)), device_id_type=MESH
        )

    rows = groups * UNIT
    second = (iota((rows, LANES), 0) & PER_WAVE) != 0

    column = iota((rows, WINDOW), 1)
    fetch.wait()

    def gather(wave):
        for j in range(owners):
            table = False
            for t in range(3):
                at = index_ref[wave * rows : (wave + 1) * rows, 3 * j + t : 3 * j + t + 1]
                table = table | (column == at)
            y0 = (7 * j) // 4
            halves = []
            for g in range(2):
                parts = []
                for ref, y, count in ((f1_ref, y0, 3), (f2_ref, y0 // 2, 2), (f3_ref, y0 // 4, 2)):
                    parts.append(ref[g, y : y + count].reshape(-1, LANES))
                halves.append(jnp.concatenate(parts, 0))
            both = jnp.dot(
                jnp.where(table, 1.0, 0.0).astype(jnp.bfloat16),
                jnp.concatenate(halves, 1),
                preferred_element_type=jnp.float32,
            )
            picked = jnp.where(second, both[:, LANES:], both[:, :LANES])
            picked = picked.reshape(2, groups // 2, UNIT, LANES).astype(jnp.bfloat16)
            s1_ref[wave, :, j % 2, j // 2] = picked[0]
            s2_ref[wave, j] = picked[1]

    def remote(src, dst, send_sem, recv_sem, device):
        return pltpu.make_async_remote_copy(
            src_ref=src,
            dst_ref=dst,
            send_sem=send_sem,
            recv_sem=recv_sem,
            device_id=device,
            device_id_type=MESH,
        )

    def all_sent(ref, wave, send_sems, recv_sems):
        part = ref.at[wave, pl.ds(0, ref.shape[1] - 1)]
        return remote(part, part, send_sems.at[wave], recv_sems.at[wave], (me + 1 - 2 * core, pos))

    def to_group(wave, d):
        to = lax.rem(me + d, groups)
        source = s1_ref.at[wave, to // 2, to % 2]
        sems = a_send.at[wave], a_recv.at[wave]
        return remote(source, r1_ref.at[wave, me], *sems, (to, pos))

    def to_owner(wave, d):
        to = lax.rem(pos + d, owners)
        sems = b_send.at[wave], b_recv.at[wave]
        return remote(s2_ref.at[wave, to], r2_ref.at[wave, pos], *sems, (me, to))

    def on_to_owner(wave, n):
        to = lax.rem(pos // 2 + n, owners // 2)
        sems = x_send.at[wave], x_recv.at[wave]
        return remote(r1_ref.at[wave, :, to], x_ref.at[wave, pos], *sems, (me, 2 * to + core))

    def on_to_group(wave, n):
        to = lax.rem(z + n, chips)
        sems = x_send.at[wave], x_recv.at[wave]
        device = (2 * to + 1 - pos % 2, pos)
        return remote(r2_ref.at[wave, :, to], x_ref.at[wave, me], *sems, device)

    def far_first(n, count):
        return count // 2 + ((n + 1) // 2) * (1 - 2 * (n % 2))

    for wave in range(WAVES):
        gather(wave)
        if wave == 0:
            pl.semaphore_wait(barrier, groups - 1 + owners - 1)

        @pl.loop(0, groups - 1)
        def _(n, wave=wave):
            to_group(wave, far_first(n, groups)).start()

        @pl.loop(0, owners - 1)
        def _(n, wave=wave):
            to_owner(wave, far_first(n, owners)).start()

    for wave in range(WAVES):
        r1_ref[wave, me] = s1_ref[wave, z, core]
        r2_ref[wave, pos] = s2_ref[wave, pos]
    tables = flatten_tables(kept)
    masks = tables[1]
    picks = jnp.where(tables[0], 1.0, 0.0).astype(jnp.bfloat16)

    for wave in range(WAVES):

        all_sent(r2_ref, wave, b_send, b_recv).wait_recv()

        @pl.loop(odd, chips)
        def _(n, wave=wave):
            on_to_group(wave, n).start()

        all_sent(r1_ref, wave, a_send, a_recv).wait_recv()

        @pl.loop(1 - odd, owners // 2)
        def _(n, wave=wave):
            on_to_owner(wave, n).start()

    @pl.when(odd == 0)
    def _():
        for wave in range(WAVES):
            x_ref[wave, pos] = r1_ref[wave, :, pos // 2]

    @pl.when(odd == 1)
    def _():
        for wave in range(WAVES):
            x_ref[wave, me] = r2_ref[wave, :, z]

    def wave_gram(wave):
        all_sent(x_ref, wave, x_send, x_recv).wait_recv()
        units = groups * owners
        x = x_ref[wave].astype(jnp.float32).reshape(units // 2, 2, UNIT, LANES)
        x = jnp.concatenate([x[:, 0], x[:, 1]], 1).reshape(units * UNIT, LANES)
        slot = iota((units * UNIT, LANES), 0) & (PER_WAVE - 1)
        spread = jnp.concatenate([jnp.where(slot == q, x, 0.0) for q in range(PER_WAVE)], 1)
        return lax.dot_general(
            x.astype(jnp.bfloat16),
            spread.astype(jnp.bfloat16),
            (((0,), (0,)), ((), ())),
            preferred_element_type=jnp.float32,
        )

    def slot_at(distance):
        return lax.rem(z + chips - distance, chips) * 2 + core

    def share(rows, origin, target, sems, send, came):
        part = out_ref.at[slot_at(origin), pl.ds(*rows)]
        device = (lax.rem(z + target, chips) * 2 + core, pos)
        return remote(part, part, z_send.at[sems, send], z_recv.at[sems, came], device)

    def pair(wave, origin):
        part = out_ref.at[slot_at(origin), pl.ds(*WHOLE[wave])]
        sems = pair_send.at[wave, origin], pair_recv.at[wave, origin]
        return remote(part, part, *sems, (z * 2 + 1 - core, pos))

    sent = []

    def begin(wave):
        for target in (2, 6, 1, 7):
            sent.append(share(WHOLE[wave], 0, target, wave, target, target))
            sent[-1].start()

    def arrive(wave, origin):
        if origin == 4:
            share(LOWER[wave], 4, 1, wave, 0, 4).wait_recv()
            share(UPPER[wave], 4, 1, wave, 0, 0).wait_recv()
        else:
            share(WHOLE[wave], origin, 1, wave, 0, origin).wait_recv()
        if origin == 2:
            sent.append(share(LOWER[wave], 2, 2, wave, 4, 4))
            sent.append(share(WHOLE[wave], 2, 1, wave, 3, 3))
        elif origin == 6:
            sent.append(share(UPPER[wave], 6, 6, wave, 0, 0))
            sent.append(share(WHOLE[wave], 6, 7, wave, 5, 5))
        if origin in (2, 6):
            sent[-2].start()
            sent[-1].start()
        pair(wave, origin).start()

    for q in range(SLOTS - 1):
        if q % PER_WAVE == 0:
            gram = wave_gram(q // PER_WAVE)
        rows = pl.ds(q * FLAT, FLAT)
        out_ref[me, rows] = packets(kept, gram, picks, masks, q % PER_WAVE)
        if q == PER_WAVE - 1:
            begin(0)
            pair(0, 0).start()
    begin(1)
    pair(1, 0).start()
    last_ref[...] = packets(kept, gram, picks, masks, PER_WAVE - 1)
    for wave in range(WAVES):
        for origin in (2, 6, 1, 7):
            arrive(wave, origin)
    for wave in range(WAVES):
        for origin in (3, 5, 4):
            arrive(wave, origin)
    for copy in sent:
        copy.wait_send()

    for wave in range(WAVES):
        all_sent(r1_ref, wave, a_send, a_recv).wait_send()
        all_sent(r2_ref, wave, b_send, b_recv).wait_send()
        all_sent(x_ref, wave, x_send, x_recv).wait_send()
    for wave in range(WAVES):
        for origin in range(chips):
            pair(wave, origin).wait()


def per_device(
    section_one,
    section_two,
    section_three,
    weight_one,
    weight_two,
    weight_three,
    gain_one,
    gain_two,
    gain_three,
    bias_one,
    bias_two,
    bias_three,
    channel_index,
    valid_count,
):
    images, side = section_one.shape[:2]
    width_one, width_two = section_one.shape[3], section_two.shape[3]
    kept = channel_index.shape[0]
    groups, owners = lax.axis_size("img"), lax.axis_size("pos")
    block = side * side // owners
    scale = (lax.iota(jnp.int32, images) < valid_count[0, 0]).astype(jnp.bfloat16)
    scale = scale[:, None, None, None]
    out_one = section_out(section_one, weight_one, gain_one, bias_one) * scale
    out_two = section_out(section_two, weight_two, gain_two, bias_two) * scale
    out_three = section_out(section_three, weight_three, gain_three, bias_three) * scale
    slots = jnp.pad(channel_index, (0, LANES - kept), constant_values=-1024)
    f1 = pick_channels(out_one, 0, slots)
    f1 = jnp.where(lax.iota(jnp.int32, LANES) == ONES, scale, f1)
    f2 = pick_channels(out_two, width_one, slots)
    f3 = pick_channels(out_three, width_one + width_two, slots)
    f1 = jnp.pad(f1, ((0, 0), (0, 1), (0, 4), (0, 0)))
    f2 = jnp.pad(f2, ((0, 0), (0, 2), (0, 2), (0, 0)))
    f3 = jnp.pad(f3, ((0, 0), (0, 1), (0, 9), (0, 0)))
    index = jnp.asarray(gather_index(side, owners, groups))
    own = SLOTS - 1
    vmem = pl.BlockSpec(memory_space=pltpu.VMEM)
    dma = pltpu.SemaphoreType.DMA
    out, last = pl.pallas_call(
        functools.partial(kernel, kept),
        out_shape=(
            jax.ShapeDtypeStruct((groups, own * FLAT, LANES), jnp.bfloat16),
            jax.ShapeDtypeStruct((FLAT, LANES), jnp.bfloat16),
        ),
        in_specs=[vmem] * 3 + [pl.BlockSpec(memory_space=pltpu.HBM)],
        out_specs=[vmem] * 2,
        scratch_shapes=[
            pltpu.VMEM(index.shape, jnp.int32),
            dma(()),
            pltpu.VMEM((WAVES, groups // 2, 2, owners // 2, UNIT, LANES), jnp.bfloat16),
            pltpu.VMEM((WAVES, owners, groups // 2, UNIT, LANES), jnp.bfloat16),
            pltpu.VMEM((WAVES, groups, owners // 2, UNIT, LANES), jnp.bfloat16),
            pltpu.VMEM((WAVES, owners, groups // 2, UNIT, LANES), jnp.bfloat16),
            pltpu.VMEM((WAVES, owners, groups, UNIT, LANES), jnp.bfloat16),
            dma((WAVES,)),
            dma((WAVES,)),
            dma((WAVES,)),
            dma((WAVES,)),
            dma((WAVES,)),
            dma((WAVES,)),
            dma((WAVES, groups // 2)),
            dma((WAVES, groups // 2)),
            dma((WAVES, groups // 2)),
            dma((WAVES, groups // 2)),
        ],
        compiler_params=pltpu.CompilerParams(
            collective_id=0, has_side_effects=True, vmem_limit_bytes=40 * 2**20
        ),
        cost_estimate=pl.CostEstimate(
            flops=800_000_000, bytes_accessed=4_000_000, transcendentals=0
        ),
        name="statistics",
    )(f1, f2, f3, index)
    packets = jnp.concatenate(
        [out.reshape(block - 1, FLAT * LANES), last.reshape(1, FLAT * LANES)]
    ).astype(jnp.float32)
    used = kept * kept
    covariance = packets[:, :used]
    end = (FLAT - 1) * LANES
    mean = packets[:, end : end + kept] + packets[:, used : used + kept]
    return (mean.T, covariance)


def solution(mesh):
    return jax.shard_map(
        per_device,
        mesh=mesh,
        in_specs=(P(("img", "pos"), None, None, None),) * 3
        + (P(),) * 10
        + (P("img", "pos"),),
        out_specs=(P(None, "pos"), P("pos", None)),
        check_vma=False,
    )
```

```python
import functools

import jax
import jax.numpy as jnp
import numpy as np
from jax import lax
from jax.experimental import pallas as pl
from jax.experimental.pallas import tpu as pltpu
from jax.sharding import PartitionSpec as P

MESH = pl.DeviceIdType.MESH
LANES = 128
ONES = 127
SLOTS = 4
WAVES = 2
PER_WAVE = SLOTS // WAVES
UNIT = 2 * PER_WAVE
FLAT = 80
WINDOW = 160
WHOLE = ((0, 2 * FLAT), (2 * FLAT, FLAT))
LOWER = ((0, FLAT), (2 * FLAT, 32))
UPPER = ((FLAT, FLAT), (2 * FLAT + 32, FLAT - 32))


def section_out(images, weight, gain, bias):
    conv = lax.conv_general_dilated(
        images,
        weight,
        (1, 1),
        "SAME",
        dimension_numbers=("NHWC", "HWIO", "NHWC"),
        preferred_element_type=jnp.float32,
    )
    return jax.nn.relu(conv * gain + bias).astype(jnp.bfloat16)


def pick_channels(section, offset, slots):
    width = section.shape[3]
    table = (slots[None, :] - offset == lax.iota(jnp.int32, width)[:, None]).astype(jnp.bfloat16)
    return jnp.einsum(
        "ihwc,ck->ihwk", section, table, preferred_element_type=jnp.float32
    ).astype(jnp.bfloat16)


def gather_index(side, blocks, sharers):
    block = side * side // blocks
    own = block // sharers
    rows = sharers * UNIT
    index = np.full((WAVES * rows, LANES), -1, np.int32)
    for j in range(blocks):
        y0 = j * block // side
        for place in range(sharers):
            half, pair = divmod(place, sharers // 2)
            i = pair * 2 + (j + half) % 2
            for q in range(SLOTS):
                wave, part = divmod(q, PER_WAVE)
                position = j * block + (i * own + q if q < own else block - 1)
                y, x = divmod(position, side)
                columns = (
                    (y - y0) * 32 + x,
                    96 + (y // 2 - y0 // 2) * 16 + x // 2,
                    128 + (y // 4 - y0 // 4) * 16 + x // 4,
                )
                for g in range(2):
                    row = wave * rows + place * UNIT + g * PER_WAVE + part
                    index[row, j * 3 : j * 3 + 3] = columns
    return index


def iota(shape, dim):
    return lax.broadcasted_iota(jnp.int32, shape, dim)


def flatten_tables(kept):
    f = iota((FLAT, LANES), 0) * LANES
    k = iota((FLAT, LANES), 1)
    picks, masks = [], []
    start = jnp.floor((f.astype(jnp.float32) + 0.5) * (1.0 / kept))
    rest = f - start.astype(jnp.int32) * kept + k
    for t in range(3):
        picks.append(((k - t) * kept <= f) & (f < (k - t + 1) * kept))
        masks.append((rest >= t * kept) & (rest < (t + 1) * kept))
    return jnp.concatenate(picks, 0), masks


def packets(kept, gram, picks, masks, q):
    raw = gram[:, q * LANES : (q + 1) * LANES]
    k = iota((LANES, LANES), 0)
    eye = jnp.where(k == iota((LANES, LANES), 1), 0.01, 0.0)
    total = raw[ONES:, ONES:]
    mean = raw[ONES:, :] / total
    cov = (raw - raw[:, ONES:] * mean) / (total - 1.0) + eye
    for bit in (4, 8, 16, 32, 64):
        cov = jnp.where(((k * kept) & bit) != 0, pltpu.roll(cov, bit, 1), cov)
    flat = jnp.dot(picks, cov.astype(jnp.bfloat16), preferred_element_type=jnp.float32)
    packet = jnp.zeros((FLAT, LANES), jnp.float32)
    for t in range(3):
        packet = packet + jnp.where(masks[t], flat[t * FLAT : (t + 1) * FLAT], 0.0)
    row, lane = iota((FLAT, LANES), 0), iota((FLAT, LANES), 1)
    edge = kept * kept % LANES
    high = mean.astype(jnp.bfloat16).astype(jnp.float32)
    low = pltpu.roll(jnp.broadcast_to(mean - high, (8, LANES)), edge, 1)[:1]
    packet = jnp.where(row == FLAT - 1, high, packet)
    packet = jnp.where((row == FLAT - 2) & (lane >= edge), low, packet)
    return packet.astype(jnp.bfloat16)


def kernel(
    kept,
    f1_ref,
    f2_ref,
    f3_ref,
    index_hbm,
    out_ref,
    last_ref,
    index_ref,
    index_sem,
    s1_ref,
    s2_ref,
    r1_ref,
    r2_ref,
    x_ref,
    a_send,
    a_recv,
    b_send,
    b_recv,
    x_send,
    x_recv,
    z_send,
    z_recv,
    pair_send,
    pair_recv,
):
    groups, owners = r1_ref.shape[1], r2_ref.shape[1]
    chips = groups // 2
    me = lax.axis_index("img")
    pos = lax.axis_index("pos")
    z, core = me // 2, me % 2
    odd = (me + pos) % 2

    fetch = pltpu.make_async_copy(index_hbm, index_ref, index_sem)
    fetch.start()
    barrier = pltpu.get_barrier_semaphore()

    @pl.loop(1, groups)
    def _(d):
        pl.semaphore_signal(
            barrier, inc=1, device_id=(lax.rem(me + d, groups), pos), device_id_type=MESH
        )

    @pl.loop(1, owners)
    def _(d):
        pl.semaphore_signal(
            barrier, inc=1, device_id=(me, lax.rem(pos + d, owners)), device_id_type=MESH
        )

    rows = groups * UNIT
    second = (iota((rows, LANES), 0) & PER_WAVE) != 0

    column = iota((rows, WINDOW), 1)
    fetch.wait()

    def gather(wave):
        for j in range(owners):
            table = False
            for t in range(3):
                at = index_ref[wave * rows : (wave + 1) * rows, 3 * j + t : 3 * j + t + 1]
                table = table | (column == at)
            y0 = (7 * j) // 4
            halves = []
            for g in range(2):
                parts = []
                for ref, y, count in ((f1_ref, y0, 3), (f2_ref, y0 // 2, 2), (f3_ref, y0 // 4, 2)):
                    parts.append(ref[g, y : y + count].reshape(-1, LANES))
                halves.append(jnp.concatenate(parts, 0))
            both = jnp.dot(
                jnp.where(table, 1.0, 0.0).astype(jnp.bfloat16),
                jnp.concatenate(halves, 1),
                preferred_element_type=jnp.float32,
            )
            picked = jnp.where(second, both[:, LANES:], both[:, :LANES])
            picked = picked.reshape(2, groups // 2, UNIT, LANES).astype(jnp.bfloat16)
            s1_ref[wave, :, j % 2, j // 2] = picked[0]
            s2_ref[wave, j] = picked[1]

    def remote(src, dst, send_sem, recv_sem, device):
        return pltpu.make_async_remote_copy(
            src_ref=src,
            dst_ref=dst,
            send_sem=send_sem,
            recv_sem=recv_sem,
            device_id=device,
            device_id_type=MESH,
        )

    def all_sent(ref, wave, send_sems, recv_sems):
        part = ref.at[wave, pl.ds(0, ref.shape[1] - 1)]
        return remote(part, part, send_sems.at[wave], recv_sems.at[wave], (me + 1 - 2 * core, pos))

    def to_group(wave, d):
        to = lax.rem(me + d, groups)
        source = s1_ref.at[wave, to // 2, to % 2]
        sems = a_send.at[wave], a_recv.at[wave]
        return remote(source, r1_ref.at[wave, me], *sems, (to, pos))

    def to_owner(wave, d):
        to = lax.rem(pos + d, owners)
        sems = b_send.at[wave], b_recv.at[wave]
        return remote(s2_ref.at[wave, to], r2_ref.at[wave, pos], *sems, (me, to))

    def on_to_owner(wave, n):
        to = lax.rem(pos // 2 + n, owners // 2)
        sems = x_send.at[wave], x_recv.at[wave]
        return remote(r1_ref.at[wave, :, to], x_ref.at[wave, pos], *sems, (me, 2 * to + core))

    def on_to_group(wave, n):
        to = lax.rem(z + n, chips)
        sems = x_send.at[wave], x_recv.at[wave]
        device = (2 * to + 1 - pos % 2, pos)
        return remote(r2_ref.at[wave, :, to], x_ref.at[wave, me], *sems, device)

    def far_first(n, count):
        return count // 2 + ((n + 1) // 2) * (1 - 2 * (n % 2))

    for wave in range(WAVES):
        gather(wave)
        if wave == 0:
            pl.semaphore_wait(barrier, groups - 1 + owners - 1)

        @pl.loop(0, groups - 1)
        def _(n, wave=wave):
            to_group(wave, far_first(n, groups)).start()

        @pl.loop(0, owners - 1)
        def _(n, wave=wave):
            to_owner(wave, far_first(n, owners)).start()

    for wave in range(WAVES):
        r1_ref[wave, me] = s1_ref[wave, z, core]
        r2_ref[wave, pos] = s2_ref[wave, pos]
    tables = flatten_tables(kept)
    masks = tables[1]
    picks = jnp.where(tables[0], 1.0, 0.0).astype(jnp.bfloat16)

    for wave in range(WAVES):

        all_sent(r2_ref, wave, b_send, b_recv).wait_recv()

        @pl.loop(odd, chips)
        def _(n, wave=wave):
            on_to_group(wave, n).start()

        all_sent(r1_ref, wave, a_send, a_recv).wait_recv()

        @pl.loop(1 - odd, owners // 2)
        def _(n, wave=wave):
            on_to_owner(wave, n).start()

    @pl.when(odd == 0)
    def _():
        for wave in range(WAVES):
            x_ref[wave, pos] = r1_ref[wave, :, pos // 2]

    @pl.when(odd == 1)
    def _():
        for wave in range(WAVES):
            x_ref[wave, me] = r2_ref[wave, :, z]

    def wave_gram(wave):
        all_sent(x_ref, wave, x_send, x_recv).wait_recv()
        units = groups * owners
        x = x_ref[wave].astype(jnp.float32).reshape(units // 2, 2, UNIT, LANES)
        x = jnp.concatenate([x[:, 0], x[:, 1]], 1).reshape(units * UNIT, LANES)
        slot = iota((units * UNIT, LANES), 0) & (PER_WAVE - 1)
        spread = jnp.concatenate([jnp.where(slot == q, x, 0.0) for q in range(PER_WAVE)], 1)
        return lax.dot_general(
            x.astype(jnp.bfloat16),
            spread.astype(jnp.bfloat16),
            (((0,), (0,)), ((), ())),
            preferred_element_type=jnp.float32,
        )

    def slot_at(distance):
        return lax.rem(z + chips - distance, chips) * 2 + core

    def share(rows, origin, target, wave, came):
        part = out_ref.at[slot_at(origin), pl.ds(*rows)]
        device = (lax.rem(z + target, chips) * 2 + core, pos)
        return remote(part, part, z_send, z_recv.at[wave, came], device)

    def pair(wave, origin):
        part = out_ref.at[slot_at(origin), pl.ds(*WHOLE[wave])]
        return remote(part, part, pair_send, pair_recv, (z * 2 + 1 - core, pos))

    def begin(wave):
        for target in (2, 6, 1, 7):
            share(WHOLE[wave], 0, target, wave, target).start()

    def arrive(wave, origin):
        if origin == 4:
            share(LOWER[wave], 4, 1, wave, 4).wait_recv()
            share(UPPER[wave], 4, 1, wave, 0).wait_recv()
        else:
            share(WHOLE[wave], origin, 1, wave, origin).wait_recv()
        if origin == 2:
            share(LOWER[wave], 2, 2, wave, 4).start()
            share(WHOLE[wave], 2, 1, wave, 3).start()
        elif origin == 6:
            share(UPPER[wave], 6, 6, wave, 0).start()
            share(WHOLE[wave], 6, 7, wave, 5).start()
        pair(wave, origin).start()

    for q in range(SLOTS - 1):
        if q % PER_WAVE == 0:
            gram = wave_gram(q // PER_WAVE)
        rows = pl.ds(q * FLAT, FLAT)
        out_ref[me, rows] = packets(kept, gram, picks, masks, q % PER_WAVE)
        if q == PER_WAVE - 1:
            begin(0)
            pair(0, 0).start()
    begin(1)
    pair(1, 0).start()
    last_ref[...] = packets(kept, gram, picks, masks, PER_WAVE - 1)
    for wave in range(WAVES):
        for origin in (2, 6, 1, 7):
            arrive(wave, origin)
    for wave in range(WAVES):
        for origin in (3, 5, 4):
            arrive(wave, origin)
    partner = (z * 2 + 1 - core, pos)
    part = out_ref.at[pl.ds(0, chips - 1)]
    remote(part, part, z_send, pair_recv, partner).wait_send()

    for wave in range(WAVES):
        all_sent(r1_ref, wave, a_send, a_recv).wait_send()
        all_sent(r2_ref, wave, b_send, b_recv).wait_send()
        all_sent(x_ref, wave, x_send, x_recv).wait_send()
    part = out_ref.at[pl.ds(0, chips)]
    remote(part, part, pair_send, pair_recv, partner).wait()


def per_device(
    section_one,
    section_two,
    section_three,
    weight_one,
    weight_two,
    weight_three,
    gain_one,
    gain_two,
    gain_three,
    bias_one,
    bias_two,
    bias_three,
    channel_index,
    valid_count,
):
    images, side = section_one.shape[:2]
    width_one, width_two = section_one.shape[3], section_two.shape[3]
    kept = channel_index.shape[0]
    groups, owners = lax.axis_size("img"), lax.axis_size("pos")
    block = side * side // owners
    scale = (lax.iota(jnp.int32, images) < valid_count[0, 0]).astype(jnp.bfloat16)
    scale = scale[:, None, None, None]
    out_one = section_out(section_one, weight_one, gain_one, bias_one) * scale
    out_two = section_out(section_two, weight_two, gain_two, bias_two) * scale
    out_three = section_out(section_three, weight_three, gain_three, bias_three) * scale
    slots = jnp.pad(channel_index, (0, LANES - kept), constant_values=-1024)
    f1 = pick_channels(out_one, 0, slots)
    f1 = jnp.where(lax.iota(jnp.int32, LANES) == ONES, scale, f1)
    f2 = pick_channels(out_two, width_one, slots)
    f3 = pick_channels(out_three, width_one + width_two, slots)
    f1 = jnp.pad(f1, ((0, 0), (0, 1), (0, 4), (0, 0)))
    f2 = jnp.pad(f2, ((0, 0), (0, 2), (0, 2), (0, 0)))
    f3 = jnp.pad(f3, ((0, 0), (0, 1), (0, 9), (0, 0)))
    index = jnp.asarray(gather_index(side, owners, groups))
    own = SLOTS - 1
    vmem = pl.BlockSpec(memory_space=pltpu.VMEM)
    dma = pltpu.SemaphoreType.DMA
    out, last = pl.pallas_call(
        functools.partial(kernel, kept),
        out_shape=(
            jax.ShapeDtypeStruct((groups, own * FLAT, LANES), jnp.bfloat16),
            jax.ShapeDtypeStruct((FLAT, LANES), jnp.bfloat16),
        ),
        in_specs=[vmem] * 3 + [pl.BlockSpec(memory_space=pltpu.HBM)],
        out_specs=[vmem] * 2,
        scratch_shapes=[
            pltpu.VMEM(index.shape, jnp.int32),
            dma(()),
            pltpu.VMEM((WAVES, groups // 2, 2, owners // 2, UNIT, LANES), jnp.bfloat16),
            pltpu.VMEM((WAVES, owners, groups // 2, UNIT, LANES), jnp.bfloat16),
            pltpu.VMEM((WAVES, groups, owners // 2, UNIT, LANES), jnp.bfloat16),
            pltpu.VMEM((WAVES, owners, groups // 2, UNIT, LANES), jnp.bfloat16),
            pltpu.VMEM((WAVES, owners, groups, UNIT, LANES), jnp.bfloat16),
            dma((WAVES,)),
            dma((WAVES,)),
            dma((WAVES,)),
            dma((WAVES,)),
            dma((WAVES,)),
            dma((WAVES,)),
            dma(()),
            dma((WAVES, groups // 2)),
            dma(()),
            dma(()),
        ],
        compiler_params=pltpu.CompilerParams(
            collective_id=0, has_side_effects=True, vmem_limit_bytes=40 * 2**20
        ),
        cost_estimate=pl.CostEstimate(
            flops=800_000_000, bytes_accessed=4_000_000, transcendentals=0
        ),
        name="statistics",
    )(f1, f2, f3, index)
    packets = jnp.concatenate(
        [out.reshape(block - 1, FLAT * LANES), last.reshape(1, FLAT * LANES)]
    ).astype(jnp.float32)
    used = kept * kept
    covariance = packets[:, :used]
    end = (FLAT - 1) * LANES
    mean = packets[:, end : end + kept] + packets[:, used : used + kept]
    return (mean.T, covariance)


def solution(mesh):
    return jax.shard_map(
        per_device,
        mesh=mesh,
        in_specs=(P(("img", "pos"), None, None, None),) * 3
        + (P(),) * 10
        + (P("img", "pos"),),
        out_specs=(P(None, "pos"), P("pos", None)),
        check_vma=False,
    )
```

```python
import functools

import jax
import jax.numpy as jnp
import numpy as np
from jax import lax
from jax.experimental import pallas as pl
from jax.experimental.pallas import tpu as pltpu
from jax.sharding import PartitionSpec as P

MESH = pl.DeviceIdType.MESH
LANES = 128
ONES = 127
SLOTS = 4
WAVES = 2
PER_WAVE = SLOTS // WAVES
UNIT = 2 * PER_WAVE
FLAT = 80
WINDOW = 160
WHOLE = ((0, 2 * FLAT), (2 * FLAT, FLAT))
LOWER = ((0, FLAT), (2 * FLAT, 32))
UPPER = ((FLAT, FLAT), (2 * FLAT + 32, FLAT - 32))


def section_out(images, weight, gain, bias):
    conv = lax.conv_general_dilated(
        images,
        weight,
        (1, 1),
        "SAME",
        dimension_numbers=("NHWC", "HWIO", "NHWC"),
        preferred_element_type=jnp.float32,
    )
    return jax.nn.relu(conv * gain + bias).astype(jnp.bfloat16)


def pick_channels(section, offset, slots):
    width = section.shape[3]
    table = (slots[None, :] - offset == lax.iota(jnp.int32, width)[:, None]).astype(jnp.bfloat16)
    return jnp.einsum(
        "ihwc,ck->ihwk", section, table, preferred_element_type=jnp.float32
    ).astype(jnp.bfloat16)


def gather_index(side, blocks, sharers):
    block = side * side // blocks
    own = block // sharers
    rows = sharers * UNIT
    index = np.full((WAVES * rows, LANES), -1, np.int32)
    for j in range(blocks):
        y0 = j * block // side
        for place in range(sharers):
            half, pair = divmod(place, sharers // 2)
            i = pair * 2 + (j + half) % 2
            for q in range(SLOTS):
                wave, part = divmod(q, PER_WAVE)
                position = j * block + (i * own + q if q < own else block - 1)
                y, x = divmod(position, side)
                columns = (
                    (y - y0) * 32 + x,
                    96 + (y // 2 - y0 // 2) * 16 + x // 2,
                    128 + (y // 4 - y0 // 4) * 16 + x // 4,
                )
                for g in range(2):
                    row = wave * rows + place * UNIT + g * PER_WAVE + part
                    index[row, j * 3 : j * 3 + 3] = columns
    return index


def iota(shape, dim):
    return lax.broadcasted_iota(jnp.int32, shape, dim)


def flatten_tables(kept):
    f = iota((FLAT, LANES), 0) * LANES
    k = iota((FLAT, LANES), 1)
    picks, masks = [], []
    start = jnp.floor((f.astype(jnp.float32) + 0.5) * (1.0 / kept))
    rest = f - start.astype(jnp.int32) * kept + k
    for t in range(3):
        picks.append(((k - t) * kept <= f) & (f < (k - t + 1) * kept))
        masks.append((rest >= t * kept) & (rest < (t + 1) * kept))
    return jnp.concatenate(picks, 0), masks


def packets(kept, gram, picks, masks, q):
    raw = gram[:, q * LANES : (q + 1) * LANES]
    k = iota((LANES, LANES), 0)
    eye = jnp.where(k == iota((LANES, LANES), 1), 0.01, 0.0)
    total = raw[ONES:, ONES:]
    mean = raw[ONES:, :] / total
    cov = (raw - raw[:, ONES:] * mean) / (total - 1.0) + eye
    for bit in (4, 8, 16, 32, 64):
        cov = jnp.where(((k * kept) & bit) != 0, pltpu.roll(cov, bit, 1), cov)
    flat = jnp.dot(picks, cov.astype(jnp.bfloat16), preferred_element_type=jnp.float32)
    packet = jnp.zeros((FLAT, LANES), jnp.float32)
    for t in range(3):
        packet = packet + jnp.where(masks[t], flat[t * FLAT : (t + 1) * FLAT], 0.0)
    row, lane = iota((FLAT, LANES), 0), iota((FLAT, LANES), 1)
    edge = kept * kept % LANES
    high = mean.astype(jnp.bfloat16).astype(jnp.float32)
    low = pltpu.roll(jnp.broadcast_to(mean - high, (8, LANES)), edge, 1)[:1]
    packet = jnp.where(row == FLAT - 1, high, packet)
    packet = jnp.where((row == FLAT - 2) & (lane >= edge), low, packet)
    return packet.astype(jnp.bfloat16)


def kernel(
    kept,
    f1_ref,
    f2_ref,
    f3_ref,
    index_hbm,
    out_ref,
    last_ref,
    index_ref,
    index_sem,
    s1_ref,
    s2_ref,
    r1_ref,
    r2_ref,
    x_ref,
    a_send,
    a_recv,
    b_send,
    b_recv,
    x_send,
    x_recv,
    z_send,
    z_recv,
    pair_send,
    pair_recv,
):
    groups, owners = r1_ref.shape[1], r2_ref.shape[1]
    chips = groups // 2
    me = lax.axis_index("img")
    pos = lax.axis_index("pos")
    z, core = me // 2, me % 2
    odd = (me + pos) % 2

    fetch = pltpu.make_async_copy(index_hbm, index_ref, index_sem)
    fetch.start()
    barrier = pltpu.get_barrier_semaphore()

    @pl.loop(1, groups)
    def _(d):
        pl.semaphore_signal(
            barrier, inc=1, device_id=(lax.rem(me + d, groups), pos), device_id_type=MESH
        )

    @pl.loop(1, owners)
    def _(d):
        pl.semaphore_signal(
            barrier, inc=1, device_id=(me, lax.rem(pos + d, owners)), device_id_type=MESH
        )

    rows = groups * UNIT
    second = (iota((rows, LANES), 0) & PER_WAVE) != 0

    column = iota((rows, WINDOW), 1)
    fetch.wait()

    def gather(wave):
        for j in range(owners):
            table = False
            for t in range(3):
                at = index_ref[wave * rows : (wave + 1) * rows, 3 * j + t : 3 * j + t + 1]
                table = table | (column == at)
            y0 = (7 * j) // 4
            halves = []
            for g in range(2):
                parts = []
                for ref, y, count in ((f1_ref, y0, 3), (f2_ref, y0 // 2, 2), (f3_ref, y0 // 4, 2)):
                    parts.append(ref[g, y : y + count].reshape(-1, LANES))
                halves.append(jnp.concatenate(parts, 0))
            both = jnp.dot(
                jnp.where(table, 1.0, 0.0).astype(jnp.bfloat16),
                jnp.concatenate(halves, 1),
                preferred_element_type=jnp.float32,
            )
            picked = jnp.where(second, both[:, LANES:], both[:, :LANES])
            picked = picked.reshape(2, groups // 2, UNIT, LANES).astype(jnp.bfloat16)
            s1_ref[wave, :, j % 2, j // 2] = picked[0]
            s2_ref[wave, j] = picked[1]

    def remote(src, dst, send_sem, recv_sem, device):
        return pltpu.make_async_remote_copy(
            src_ref=src,
            dst_ref=dst,
            send_sem=send_sem,
            recv_sem=recv_sem,
            device_id=device,
            device_id_type=MESH,
        )

    def all_sent(ref, wave, send_sems, recv_sems):
        part = ref.at[wave, pl.ds(0, ref.shape[1] - 1)]
        return remote(part, part, send_sems.at[wave], recv_sems.at[wave], (me + 1 - 2 * core, pos))

    def to_group(wave, d):
        to = lax.rem(me + d, groups)
        source = s1_ref.at[wave, to // 2, to % 2]
        sems = a_send.at[wave], a_recv.at[wave]
        return remote(source, r1_ref.at[wave, me], *sems, (to, pos))

    def to_owner(wave, d):
        to = lax.rem(pos + d, owners)
        sems = b_send.at[wave], b_recv.at[wave]
        return remote(s2_ref.at[wave, to], r2_ref.at[wave, pos], *sems, (me, to))

    def on_to_owner(wave, n):
        to = lax.rem(pos // 2 + n, owners // 2)
        sems = x_send.at[wave], x_recv.at[wave]
        return remote(r1_ref.at[wave, :, to], x_ref.at[wave, pos], *sems, (me, 2 * to + core))

    def on_to_group(wave, n):
        to = lax.rem(z + n, chips)
        sems = x_send.at[wave], x_recv.at[wave]
        device = (2 * to + 1 - pos % 2, pos)
        return remote(r2_ref.at[wave, :, to], x_ref.at[wave, me], *sems, device)

    def far_first(n, count):
        return count // 2 + ((n + 1) // 2) * (1 - 2 * (n % 2))

    for wave in range(WAVES):
        gather(wave)
        if wave == 0:
            pl.semaphore_wait(barrier, groups - 1 + owners - 1)

        @pl.loop(0, groups - 1)
        def _(n, wave=wave):
            to_group(wave, far_first(n, groups)).start()

        @pl.loop(0, owners - 1)
        def _(n, wave=wave):
            to_owner(wave, far_first(n, owners)).start()

    for wave in range(WAVES):
        r1_ref[wave, me] = s1_ref[wave, z, core]
        r2_ref[wave, pos] = s2_ref[wave, pos]
    tables = flatten_tables(kept)
    masks = tables[1]
    picks = jnp.where(tables[0], 1.0, 0.0).astype(jnp.bfloat16)

    for wave in range(WAVES):

        all_sent(r2_ref, wave, b_send, b_recv).wait_recv()

        @pl.loop(odd, chips)
        def _(n, wave=wave):
            on_to_group(wave, n).start()

        all_sent(r1_ref, wave, a_send, a_recv).wait_recv()

        @pl.loop(1 - odd, owners // 2)
        def _(n, wave=wave):
            on_to_owner(wave, n).start()

    @pl.when(odd == 0)
    def _():
        for wave in range(WAVES):
            x_ref[wave, pos] = r1_ref[wave, :, pos // 2]

    @pl.when(odd == 1)
    def _():
        for wave in range(WAVES):
            x_ref[wave, me] = r2_ref[wave, :, z]

    def wave_gram(wave):
        all_sent(x_ref, wave, x_send, x_recv).wait_recv()
        units = groups * owners
        x = x_ref[wave].astype(jnp.float32).reshape(units // 2, 2, UNIT, LANES)
        x = jnp.concatenate([x[:, 0], x[:, 1]], 1).reshape(units * UNIT, LANES)
        slot = iota((units * UNIT, LANES), 0) & (PER_WAVE - 1)
        spread = jnp.concatenate([jnp.where(slot == q, x, 0.0) for q in range(PER_WAVE)], 1)
        return lax.dot_general(
            x.astype(jnp.bfloat16),
            spread.astype(jnp.bfloat16),
            (((0,), (0,)), ((), ())),
            preferred_element_type=jnp.float32,
        )

    def slot_at(distance):
        return lax.rem(z + chips - distance, chips) * 2 + core

    def share(rows, origin, target, wave, came):
        part = out_ref.at[slot_at(origin), pl.ds(*rows)]
        device = (lax.rem(z + target, chips) * 2 + core, pos)
        return remote(part, part, z_send, z_recv.at[wave, came], device)

    def pair(wave, origin):
        part = out_ref.at[slot_at(origin), pl.ds(*WHOLE[wave])]
        return remote(part, part, pair_send, pair_recv, (z * 2 + 1 - core, pos))

    def begin(wave):
        for target in (2, 6, 1, 7):
            share(WHOLE[wave], 0, target, wave, target).start()

    def arrive(wave, origin):
        if origin == 4:
            share(LOWER[wave], 4, 1, wave, 4).wait_recv()
            share(UPPER[wave], 4, 1, wave, 0).wait_recv()
        else:
            share(WHOLE[wave], origin, 1, wave, origin).wait_recv()
        if origin == 2:
            share(LOWER[wave], 2, 2, wave, 4).start()
            share(WHOLE[wave], 2, 1, wave, 3).start()
        elif origin == 6:
            share(UPPER[wave], 6, 6, wave, 0).start()
            share(WHOLE[wave], 6, 7, wave, 5).start()
        pair(wave, origin).start()

    for q in range(SLOTS - 1):
        if q % PER_WAVE == 0:
            gram = wave_gram(q // PER_WAVE)
        rows = pl.ds(q * FLAT, FLAT)
        out_ref[me, rows] = packets(kept, gram, picks, masks, q % PER_WAVE)
        if q == PER_WAVE - 1:
            begin(0)
            pair(0, 0).start()
    begin(1)
    pair(1, 0).start()
    for wave in range(WAVES):
        for origin in (2, 6, 1, 7):
            arrive(wave, origin)
    last_ref[...] = packets(kept, gram, picks, masks, PER_WAVE - 1)
    for wave in range(WAVES):
        for origin in (3, 5, 4):
            arrive(wave, origin)
    partner = (z * 2 + 1 - core, pos)
    part = out_ref.at[pl.ds(0, chips - 1)]
    remote(part, part, z_send, pair_recv, partner).wait_send()

    for wave in range(WAVES):
        all_sent(r1_ref, wave, a_send, a_recv).wait_send()
        all_sent(r2_ref, wave, b_send, b_recv).wait_send()
        all_sent(x_ref, wave, x_send, x_recv).wait_send()
    part = out_ref.at[pl.ds(0, chips)]
    remote(part, part, pair_send, pair_recv, partner).wait()


def per_device(
    section_one,
    section_two,
    section_three,
    weight_one,
    weight_two,
    weight_three,
    gain_one,
    gain_two,
    gain_three,
    bias_one,
    bias_two,
    bias_three,
    channel_index,
    valid_count,
):
    images, side = section_one.shape[:2]
    width_one, width_two = section_one.shape[3], section_two.shape[3]
    kept = channel_index.shape[0]
    groups, owners = lax.axis_size("img"), lax.axis_size("pos")
    block = side * side // owners
    scale = (lax.iota(jnp.int32, images) < valid_count[0, 0]).astype(jnp.bfloat16)
    scale = scale[:, None, None, None]
    out_one = section_out(section_one, weight_one, gain_one, bias_one) * scale
    out_two = section_out(section_two, weight_two, gain_two, bias_two) * scale
    out_three = section_out(section_three, weight_three, gain_three, bias_three) * scale
    slots = jnp.pad(channel_index, (0, LANES - kept), constant_values=-1024)
    f1 = pick_channels(out_one, 0, slots)
    f1 = jnp.where(lax.iota(jnp.int32, LANES) == ONES, scale, f1)
    f2 = pick_channels(out_two, width_one, slots)
    f3 = pick_channels(out_three, width_one + width_two, slots)
    f1 = jnp.pad(f1, ((0, 0), (0, 1), (0, 4), (0, 0)))
    f2 = jnp.pad(f2, ((0, 0), (0, 2), (0, 2), (0, 0)))
    f3 = jnp.pad(f3, ((0, 0), (0, 1), (0, 9), (0, 0)))
    index = jnp.asarray(gather_index(side, owners, groups))
    own = SLOTS - 1
    vmem = pl.BlockSpec(memory_space=pltpu.VMEM)
    dma = pltpu.SemaphoreType.DMA
    out, last = pl.pallas_call(
        functools.partial(kernel, kept),
        out_shape=(
            jax.ShapeDtypeStruct((groups, own * FLAT, LANES), jnp.bfloat16),
            jax.ShapeDtypeStruct((FLAT, LANES), jnp.bfloat16),
        ),
        in_specs=[vmem] * 3 + [pl.BlockSpec(memory_space=pltpu.HBM)],
        out_specs=[vmem] * 2,
        scratch_shapes=[
            pltpu.VMEM(index.shape, jnp.int32),
            dma(()),
            pltpu.VMEM((WAVES, groups // 2, 2, owners // 2, UNIT, LANES), jnp.bfloat16),
            pltpu.VMEM((WAVES, owners, groups // 2, UNIT, LANES), jnp.bfloat16),
            pltpu.VMEM((WAVES, groups, owners // 2, UNIT, LANES), jnp.bfloat16),
            pltpu.VMEM((WAVES, owners, groups // 2, UNIT, LANES), jnp.bfloat16),
            pltpu.VMEM((WAVES, owners, groups, UNIT, LANES), jnp.bfloat16),
            dma((WAVES,)),
            dma((WAVES,)),
            dma((WAVES,)),
            dma((WAVES,)),
            dma((WAVES,)),
            dma((WAVES,)),
            dma(()),
            dma((WAVES, groups // 2)),
            dma(()),
            dma(()),
        ],
        compiler_params=pltpu.CompilerParams(
            collective_id=0, has_side_effects=True, vmem_limit_bytes=40 * 2**20
        ),
        cost_estimate=pl.CostEstimate(
            flops=800_000_000, bytes_accessed=4_000_000, transcendentals=0
        ),
        name="statistics",
    )(f1, f2, f3, index)
    packets = jnp.concatenate(
        [out.reshape(block - 1, FLAT * LANES), last.reshape(1, FLAT * LANES)]
    ).astype(jnp.float32)
    used = kept * kept
    covariance = packets[:, :used]
    end = (FLAT - 1) * LANES
    mean = packets[:, end : end + kept] + packets[:, used : used + kept]
    return (mean.T, covariance)


def solution(mesh):
    return jax.shard_map(
        per_device,
        mesh=mesh,
        in_specs=(P(("img", "pos"), None, None, None),) * 3
        + (P(),) * 10
        + (P("img", "pos"),),
        out_specs=(P(None, "pos"), P("pos", None)),
        check_vma=False,
    )
```
